256 devices in a mesh: rep: 16 (over x, y_hi, core), fsdp: 16 (over y_lo, z).
Axes of the slice: x: 4, y: 4 (y_hi: 2, y_lo: 2; y = y_hi * 2 + y_lo), z: 8, core: 2. Of those that a mesh axis runs over, the one named last changes fastest.
Arguments:
- activations: bfloat16 [65536, 4096], P(('rep', 'fsdp')), may hold values from -200 to 200
- queries: bfloat16 [65536, 4096], P(('rep', 'fsdp')), may hold values from -18 to 18
- attention_output_cotangent: bfloat16 [65536, 4096], P(('rep', 'fsdp')), may hold values from -4 to 4
- document_ids: int32 [256, 256], P(('rep', 'fsdp')), may hold values from 0 to 3, never falling along the last dimension, each value on 1 to 128 neighbouring positions
- norm_gain: bfloat16 [16, 4096], P('rep', 'fsdp'), may hold values from 0.5 to 1.5
- key_value_weight: bfloat16 [16, 4096, 1024], P('rep', 'fsdp'), may hold values from -0.09375 to 0.09375
- fragment_local: bfloat16 [16, 4096, 1024], P('rep', 'fsdp'), may hold values from -6 to 6
- fragment_master: float32 [4096, 1024], P('fsdp', 'rep'), may hold values from -6 to 6
- fragment_moment: float32 [4096, 1024], P('fsdp', 'rep'), may hold values from -6 to 6
Outputs:
- query_gradient: bfloat16 [65536, 4096], P(('rep', 'fsdp'))
- input_gradient: bfloat16 [65536, 4096], P(('rep', 'fsdp'))
- weight_gradient: float32 [16, 4096, 1024], P('rep', 'fsdp')
- gain_gradient: float32 [16, 4096], P('rep', 'fsdp')
- master_next: float32 [4096, 1024], P('fsdp', 'rep')
- moment_next: float32 [4096, 1024], P('fsdp', 'rep')
- fragment_next: bfloat16 [16, 4096, 1024], P('rep', 'fsdp')
The draws below stay inside these ranges and needn't reach their ends.
Inputs may be any that keep to these rules, and one draw needn't show every extreme that they name: `document_ids`: along each row the numbers never fall; every number from 0 to 3 appears in every row, on at most 128 tokens.
All inputs are finite; a program needn't handle non-finite values.
Results may differ from the reference program's by a relative error of at most 0.023.
Values may be sent and summed in bfloat16 or wider, within the bound.
A program may use at most 128 MiB of HBM per device.

```python
import math
import jax
import jax.numpy as jnp
import numpy as np
from jax import lax

D = 4096
QUERY_HEADS = 32
KEY_VALUE_HEADS = 4
HEAD_DIMENSION = 128
TOK_DEV = 256
DOCS = 4
QW = 4096
KVW = 1024
NSEQ = 256
TOKENS = 65536
N_REP = 16
N_FSDP = 16


def draw_activations(key, part):
    key = jax.random.fold_in(key, 11)
    value_rows = jax.random.truncated_normal(jax.random.fold_in(key, 1), -6.0, 6.0, (TOKENS, D), jnp.float32)
    return value_rows.astype(jnp.bfloat16)


def draw_queries(key, part):
    key = jax.random.fold_in(key, 23)
    value_rows = jax.random.truncated_normal(jax.random.fold_in(key, 1), -4.5, 4.5, (TOKENS, QW), jnp.float32)
    return value_rows.astype(jnp.bfloat16)


def block_levels(stream_key, dims, split, smallest, top_value):
    factor_of, own = 1.0, jax.random.fold_in(stream_key, 6)
    for dim, blocks in split:
        steps = jnp.exp(jax.random.uniform(jax.random.fold_in(own, dim), (blocks,), jnp.float32, smallest / len(split), top_value / len(split)))
        factor_of = factor_of * jnp.repeat(steps, dims[dim] // blocks).reshape([-1 if axis == dim else 1 for axis in range(len(dims))])
    return factor_of


def profile(count, total, bound, skew):
    loads = [(1 << 20) // math.isqrt(standing ** skew) + 1 for standing in range(2, count + 1)]
    spare, holding = total - bound - (count - 1), [1] * (count - 1)
    while spare > 0:
        movable = [i for i in range(count - 1) if holding[i] < bound]
        whole, budget = sum([loads[i] for i in movable]), spare
        for i in movable:
            addition = min(bound - holding[i], max(1, budget * loads[i] // whole), spare)
            holding[i] = holding[i] + addition
            spare = spare - addition
    return np.array([bound] + holding)


def ragged_sizes(own_key, amount, total, most, lean):
    if amount == 2:
        one = jax.random.randint(own_key, (), max(1, total - most), min(most, total - 1) + 1)
        return jnp.stack([one, total - one])
    lengths = jnp.asarray(profile(amount, total, most, lean), jnp.int32)
    twos = (amount - 1) // 2
    donor, taker = lengths[1:1 + 2 * twos:2], lengths[2:2 + 2 * twos:2]
    room = jnp.minimum(donor - 1, most - taker)
    shifted = jax.random.randint(jax.random.fold_in(own_key, 1), (twos,), 0, 1 << 20) % (room + 1)
    lengths = lengths.at[1:1 + 2 * twos:2].set(donor - shifted).at[2:2 + 2 * twos:2].set(taker + shifted)
    return lengths[jax.random.permutation(jax.random.fold_in(own_key, 2), amount)]


def scatter_about(own_key, shape, spread, most, pieces=(), held_as=jnp.bfloat16):
    level = block_levels(own_key, shape, pieces, -0.22, 0.18) if pieces else 1.0
    entries = jax.random.normal(own_key, shape, jnp.float32) * spread * level
    return jnp.minimum(jnp.maximum(entries, -most), most).astype(held_as)


def setup_inputs(seed: int = 0) -> dict:
    splits = jax.random.split(jax.random.key(seed), 10)
    activations = draw_activations(jax.random.fold_in(splits[9], 71), 0)
    queries = draw_queries(jax.random.fold_in(splits[9], 71), 0)
    attention_output_cotangent = scatter_about(splits[2], (TOKENS, QW), 0.25, 4.0, ((0, 256),))
    document_ids = jax.vmap(lambda own: jnp.searchsorted(jnp.cumsum(ragged_sizes(own, DOCS, TOK_DEV, TOK_DEV // 2, 1)), jnp.arange(TOK_DEV), side="right"))(jax.random.split(splits[3], NSEQ)).reshape((NSEQ, TOK_DEV)).astype(jnp.int32)
    norm_gain = jnp.clip(1.0 + 0.1 * jax.random.normal(splits[4], (N_REP, D), jnp.float32), 0.5, 1.5).astype(jnp.bfloat16)
    key_value_weight = scatter_about(splits[5], (N_REP, D, KVW), D ** -0.5, 0.09375, ((0, 16), (1, 16)))
    fragment_local = scatter_about(splits[6], (N_REP, D, KVW), 1.0, 6.0, ((0, 16), (1, 16)))
    fragment_master = scatter_about(splits[7], (D, KVW), 1.0, 6.0, ((0, 16), (1, 16)), jnp.float32)
    fragment_moment = scatter_about(splits[8], (D, KVW), 0.5, 6.0, ((0, 16), (1, 16)), jnp.float32)
    return {"activations": activations, "queries": queries, "attention_output_cotangent": attention_output_cotangent, "document_ids": document_ids, "norm_gain": norm_gain, "key_value_weight": key_value_weight, "fragment_local": fragment_local, "fragment_master": fragment_master, "fragment_moment": fragment_moment}


epsilon = 1e-05
rope_base = 500000.0
outer_rate = 0.7
outer_momentum = 0.9
mixing = 0.5
masked_score = -1e+30

def rounded_halfway(block):
    return lax.optimization_barrier(block.astype(jnp.bfloat16))

def doc_positions(document_row):
    sequence_length = document_row.shape[0]
    index = jnp.arange(sequence_length, dtype=jnp.int32)
    changed = jnp.concatenate([jnp.ones((1,), jnp.int32), (document_row[1:] != document_row[:-1]).astype(jnp.int32)])
    first = lax.cummax(jnp.where(changed > 0, index, jnp.zeros_like(index)), axis=0)
    return index - first

def rope_tables(document_row):
    half = HEAD_DIMENSION // 2
    frequency = jnp.power(jnp.float32(rope_base), -2.0 * jnp.arange(half, dtype=jnp.float32) / HEAD_DIMENSION)
    angle = doc_positions(document_row).astype(jnp.float32)[:, None] * frequency[None, :]
    cosine = jnp.concatenate([jnp.cos(angle), jnp.cos(angle)], axis=1)
    sine = jnp.concatenate([jnp.sin(angle), jnp.sin(angle)], axis=1)
    return (cosine[:, None, :], sine[:, None, :])

def rotate(block):
    half = block.shape[-1] // 2
    return jnp.concatenate([-block[..., half:], block[..., :half]], axis=-1)

def rotate_back(block):
    half = block.shape[-1] // 2
    return jnp.concatenate([block[..., half:], -block[..., :half]], axis=-1)

def sequence_terms(tokens, rows_of_query, rows_cotangent, document_row, gain, weight):
    sequence_length = tokens.shape[0]
    query_group = QUERY_HEADS // KEY_VALUE_HEADS
    scale = HEAD_DIMENSION ** (-0.5)
    wide = tokens.astype(jnp.float32)
    inverse = lax.rsqrt(lax.optimization_barrier(jnp.mean(wide * wide, axis=1, keepdims=True)) + epsilon)
    normed = (wide * inverse * gain.astype(jnp.float32)).astype(jnp.bfloat16)
    key_value_pair = jnp.dot(normed, weight, preferred_element_type=jnp.float32)
    cosine, sine = rope_tables(document_row)
    key_unprocessed = key_value_pair[:, :KEY_VALUE_HEADS * HEAD_DIMENSION].reshape(sequence_length, KEY_VALUE_HEADS, HEAD_DIMENSION)
    keys = rounded_halfway(key_unprocessed * cosine + rotate(key_unprocessed) * sine).astype(jnp.float32)
    value_rows = rounded_halfway(key_value_pair[:, KEY_VALUE_HEADS * HEAD_DIMENSION:].reshape(sequence_length, KEY_VALUE_HEADS, HEAD_DIMENSION)).astype(jnp.float32)
    heads_of_query = rows_of_query.reshape(sequence_length, KEY_VALUE_HEADS, query_group, HEAD_DIMENSION).astype(jnp.float32)
    heads_cotangent = rows_cotangent.reshape(sequence_length, KEY_VALUE_HEADS, query_group, HEAD_DIMENSION).astype(jnp.float32)
    index = jnp.arange(sequence_length, dtype=jnp.int32)
    allowed = (index[None, :] <= index[:, None]) & (document_row[None, :] == document_row[:, None])
    scores = jnp.einsum('tkgd,skd->kgts', heads_of_query, keys) * scale
    scores = jnp.where(allowed, scores, masked_score)
    highest = lax.optimization_barrier(jnp.max(scores, axis=3, keepdims=True))
    exponent = jnp.exp(scores - highest)
    attention_weights = exponent / lax.optimization_barrier(jnp.sum(exponent, axis=3, keepdims=True))
    weights_half = rounded_halfway(attention_weights).astype(jnp.float32)
    weight_cotangent = jnp.einsum('tkgd,skd->kgts', heads_cotangent, value_rows)
    row_delta = lax.optimization_barrier(jnp.sum(attention_weights * weight_cotangent, axis=3, keepdims=True))
    score_cotangent = rounded_halfway(attention_weights * (weight_cotangent - row_delta) * scale).astype(jnp.float32)
    query_gradient = jnp.einsum('kgts,skd->tkgd', score_cotangent, keys).astype(jnp.bfloat16).reshape(sequence_length, QUERY_HEADS * HEAD_DIMENSION)
    key_cotangent = jnp.einsum('kgts,tkgd->skd', score_cotangent, heads_of_query)
    cotangent_of_value = jnp.einsum('kgts,tkgd->skd', weights_half, heads_cotangent)
    unrotated_key = key_cotangent * cosine + rotate_back(key_cotangent * sine)
    cotangent_of_projection = jnp.concatenate([unrotated_key.reshape(sequence_length, KEY_VALUE_HEADS * HEAD_DIMENSION), cotangent_of_value.reshape(sequence_length, KEY_VALUE_HEADS * HEAD_DIMENSION)], axis=1).astype(jnp.bfloat16)
    weight_term = lax.dot_general(normed, cotangent_of_projection, (((0,), (0,)), ((), ())), preferred_element_type=jnp.float32)
    normed_gradient = lax.dot_general(cotangent_of_projection, weight, (((1,), (1,)), ((), ())), preferred_element_type=jnp.float32)
    gain_term = lax.optimization_barrier(jnp.sum(normed_gradient * wide * inverse, axis=0))
    upstream = normed_gradient * gain.astype(jnp.float32)
    input_gradient = (inverse * (upstream - wide * inverse * inverse * lax.optimization_barrier(jnp.mean(upstream * wide, axis=1, keepdims=True)))).astype(jnp.bfloat16)
    return (query_gradient, input_gradient, weight_term, gain_term)

def reference(activations, queries, attention_output_cotangent, document_ids, norm_gain, key_value_weight, fragment_local, fragment_master, fragment_moment):

    def replica(replica_index):
        gain = norm_gain[replica_index]
        weight = key_value_weight[replica_index]

        def member_step(totals, member):
            row = replica_index * N_FSDP + member
            start = row * TOK_DEV
            tokens = lax.dynamic_slice_in_dim(activations, start, TOK_DEV, 0)
            rows_of_query = lax.dynamic_slice_in_dim(queries, start, TOK_DEV, 0)
            rows_cotangent = lax.dynamic_slice_in_dim(attention_output_cotangent, start, TOK_DEV, 0)
            document_row = lax.dynamic_index_in_dim(document_ids, row, 0, keepdims=False)
            query_gradient, input_gradient, weight_term, gain_term = sequence_terms(tokens, rows_of_query, rows_cotangent, document_row, gain, weight)
            weight_total = totals[0] + rounded_halfway(weight_term).astype(jnp.float32)
            gain_total = totals[1] + rounded_halfway(gain_term).astype(jnp.float32)
            return ((weight_total, gain_total), (query_gradient, input_gradient))
        start_totals = (jnp.zeros((D, KVW), jnp.float32), jnp.zeros((D,), jnp.float32))
        return lax.scan(member_step, start_totals, jnp.arange(N_FSDP, dtype=jnp.int32))
    (weight_gradient, gain_gradient), (query_rows_all, input_rows_all) = lax.map(replica, jnp.arange(N_REP, dtype=jnp.int32))

    def add_replica(index, total):
        return total + fragment_local[index].astype(jnp.float32)
    total = lax.fori_loop(0, N_REP, add_replica, jnp.zeros(fragment_master.shape, jnp.float32))
    replica_mean = total / N_REP
    pseudo = fragment_master - replica_mean
    moment_next = outer_momentum * fragment_moment + pseudo
    master_next = fragment_master - outer_rate * (pseudo + outer_momentum * moment_next)
    master_half = rounded_halfway(master_next).astype(jnp.float32)

    def merge_replica(local):
        return (mixing * local.astype(jnp.float32) + (1.0 - mixing) * master_half).astype(jnp.bfloat16)
    fragment_next = lax.map(merge_replica, fragment_local)
    return (query_rows_all.reshape(TOKENS, QW), input_rows_all.reshape(TOKENS, D), weight_gradient, gain_gradient, master_next, moment_next, fragment_next)
```

```python
import math

import jax
import jax.numpy as jnp
from jax import lax
from jax.experimental import pallas as pl
from jax.experimental.pallas import tpu as pltpu
from jax.sharding import PartitionSpec as P

epsilon = 1e-05
rope_base = 500000.0
outer_rate = 0.7
outer_momentum = 0.9
mixing = 0.5
masked_score = -1e30

TOK = 256
WIDE = 4096
HALF = 2048
GROUPS = 4
PAIRS = 4
HD = 128
RING = 8
SCALE = HD ** (-0.5)
EXP2_SCALE = SCALE * math.log2(math.e)
PIECE = 512
PIECES = HALF // PIECE

f32 = jnp.float32
bf16 = jnp.bfloat16
NT = (((1,), (1,)), ((), ()))


def dot(a, b):
    return jnp.dot(a, b, preferred_element_type=f32)


def dot_nt(a, b):
    return lax.dot_general(a, b, NT, preferred_element_type=f32)


def kernel(
    x_ref, q_ref, do_ref, doc_ref, gain_ref, w_ref, fl_ref, fm_ref, fmo_ref,
    dq_out, dx_out, dw_out, dg_out, mn_out, mo_out, fn_out,
    X, XO, XT, Q, DO, WR, WB, PIN, POUT, PRAW, E, UOUT, UIN, DX, RB, SB, DW,
    INV, CO, COS, SIN, BLO, BHI, KB, VB, KT, DKA, DVA, GC, DG,
    F, FS, FSUM, XR, YS, YR, MW, FN, M0, M1, MB, MSB, R1, R2, MN, MO,
    ag_s, ag_r, rs_s, rs_r, x_s, x_r, p_s, p_r, e_s, e_r, u_s, u_r, o_s, o_r, l_s,
):
    f = lax.axis_index("fsdp")
    r = lax.axis_index("rep")
    z = lax.rem(f, RING)
    h = lax.div(f, RING)
    core = lax.rem(r, 2)
    yh = lax.rem(lax.div(r, 2), 2)
    xx = lax.div(r, 4)

    right = {"fsdp": h * RING + lax.rem(z + 1, RING)}
    left = {"fsdp": h * RING + lax.rem(z + RING - 1, RING)}
    partner = {"fsdp": (1 - h) * RING + z}
    sibling = {"rep": xx * 4 + yh * 2 + (1 - core)}
    across = {"rep": xx * 4 + (1 - yh) * 2 + core}
    xpeer = [{"rep": lax.rem(xx + j, 4) * 4 + yh * 2 + core} for j in (1, 2, 3)]

    def remote(src, dst, ssem, rsem, device):
        return pltpu.make_async_remote_copy(
            src_ref=src, dst_ref=dst, send_sem=ssem, recv_sem=rsem,
            device_id=device, device_id_type=pl.DeviceIdType.MESH,
        )

    def al(value, m):
        return pl.multiple_of(value, m)

    mine = pl.ds(al(h * HALF, HALF), HALF)
    other = pl.ds(al((1 - h) * HALF, HALF), HALF)
    ld_w = pltpu.make_async_copy(w_ref.at[0], WR, l_s.at[0])
    ld_x = pltpu.make_async_copy(x_ref.at[:, mine], X.at[0:TOK], l_s.at[1])
    ld_xo = pltpu.make_async_copy(x_ref.at[:, other], XO, l_s.at[2])
    ld_q = pltpu.make_async_copy(q_ref, Q, l_s.at[3])
    ld_do = pltpu.make_async_copy(do_ref, DO, l_s.at[4])
    ld_f = pltpu.make_async_copy(fl_ref.at[0], F, l_s.at[5])
    ld_m0 = pltpu.make_async_copy(fm_ref, M0, l_s.at[6])
    ld_m1 = pltpu.make_async_copy(fmo_ref, M1, l_s.at[7])
    for c in (ld_w, ld_x, ld_xo, ld_f, ld_m0, ld_m1, ld_q, ld_do):
        c.start()

    barrier = pltpu.get_barrier_semaphore()
    for d in (left, right, partner, sibling, across, *xpeer):
        pl.semaphore_signal(barrier, inc=1, device_id=d, device_id_type=pl.DeviceIdType.MESH)
    pl.semaphore_wait(barrier, 8)

    def x_copy(j):
        return remote(
            x_ref.at[:, pl.ds(al((1 - h) * HALF + j * PIECE, PIECE), PIECE)],
            X.at[TOK : 2 * TOK, j * PIECE : (j + 1) * PIECE],
            x_s.at[j], x_r.at[j], partner,
        )

    for j in range(PIECES):
        x_copy(j).start()

    def ring_at(dist):
        return lax.rem(z + dist + 2 * RING, RING)

    def ag_sem(d, g, s):
        return d * 16 + g * 4 + (s - 1)

    def ag_copy(d, g, s, shard):
        start, size = (shard * TOK, TOK) if s < 4 else (shard * TOK + d * 128, 128)
        block = WB.at[g, pl.ds(al(start, 128), size)]
        i = ag_sem(d, g, s)
        return remote(block, block, ag_s.at[i], ag_r.at[i], (right, left)[d])

    def ag_send(d, g, s):
        return ag_copy(d, g, s, ring_at((1 - s) if d == 0 else (s - 1)))

    def ag_recv(d, g, s):
        return ag_copy(d, g, s, ring_at(-s if d == 0 else s))

    def ag_step(g, s):
        for d in (0, 1):
            ag_recv(d, g, s).wait_recv()
            if s < 4:
                ag_send(d, g, s + 1).start()

    eye = lax.broadcasted_iota(jnp.int32, (TOK, TOK), 0) == lax.broadcasted_iota(jnp.int32, (TOK, TOK), 1)

    def column(row):
        square = jnp.where(eye, jnp.broadcast_to(row, (TOK, TOK)), 0.0).astype(bf16)
        return dot(square, jnp.ones((TOK, HD), bf16))

    gain_row = gain_ref[...].astype(f32)
    gain = column(gain_row)
    GC[...] = gain
    ld_w.wait()
    own_rows = pl.ds(al(z * TOK, TOK), TOK)

    def scale_w(g):
        WB[g, own_rows, 0:HD] = (WR[:, g * HD : (g + 1) * HD].astype(f32) * gain).astype(bf16)
        WB[g, own_rows, HD : 2 * HD] = (
            WR[:, 512 + g * HD : 512 + (g + 1) * HD].astype(f32) * gain
        ).astype(bf16)

    for g in (0, 1):
        scale_w(g)
        for d in (0, 1):
            ag_send(d, g, 1).start()
    for g in (2, 3):
        scale_w(g)

    rows_k = pl.ds(al(core * 128, 128), 128)
    rows_o = pl.ds(al((1 - core) * 128, 128), 128)
    lane = lax.broadcasted_iota(jnp.int32, (128, 128), 1)
    low = lane < 64
    block_c = pl.ds(al((2 * xx + yh) * 128, 128), 128)
    block_x = pl.ds(al(xx * 256, 256), 256)

    def swap(v):
        return pltpu.roll(v, 64, 1)

    o_frag = remote(F.at[rows_o], FS, o_s.at[0], o_r.at[0], sibling)
    o_state = remote(MB.at[rows_o], MSB, o_s.at[1], o_r.at[1], sibling)

    def o_x(j):
        to = lax.rem(xx + j + 1, 4)
        return remote(
            FSUM.at[:, pl.ds(al(to * 256, 256), 256)], XR.at[j], o_s.at[2 + j], o_r.at[2 + j], xpeer[j]
        )

    o_y = remote(YS, YR, o_s.at[5], o_r.at[5], across)
    o_pack = remote(R1, R2, o_s.at[6], o_r.at[6], sibling)

    def mw(rows, cols, i, device):
        return remote(MW.at[rows, cols], MW.at[rows, cols], o_s.at[i], o_r.at[i], device)

    o_back_y = mw(rows_k, block_c, 7, across)
    block_c_across = pl.ds(al((2 * xx + 1 - yh) * 128, 128), 128)
    o_back_y_in = mw(rows_k, block_c_across, 7, across)

    def o_back_x(j):
        return mw(rows_k, block_x, 8 + j, xpeer[j])

    def o_back_x_in(j):
        frm = lax.rem(xx + 4 - (j + 1), 4)
        return mw(rows_k, pl.ds(al(frm * 256, 256), 256), 8 + j, xpeer[j])

    o_back_s = mw(rows_k, slice(None), 11, sibling)
    o_back_s_in = mw(rows_o, slice(None), 11, sibling)

    def outer_1():
        ld_f.wait()
        ld_m0.wait()
        ld_m1.wait()
        MB[...] = jnp.concatenate([M0[...], M1[...]], axis=1)
        o_frag.start()
        o_state.start()

    def outer_2():
        o_frag.wait_recv()
        FSUM[...] = (F[rows_k, :].astype(f32) + FS[...].astype(f32)).astype(bf16)
        for j in range(3):
            o_x(j).start()

    def outer_3():
        for j in range(3):
            o_x(j).wait_recv()
        total = FSUM[:, block_x].astype(f32)
        for j in range(3):
            total = total + XR[j].astype(f32)
        first, second = total[:, 0:128], total[:, 128:256]
        YS[...] = jnp.where(yh == 0, second, first).astype(bf16)
        R1[...] = jnp.where(yh == 0, first, second)
        o_y.start()

    def outer_4():
        o_y.wait_recv()
        o_state.wait_recv()
        mean = (R1[...] + YR[...].astype(f32)) * (1.0 / 16.0)
        own, sib = MB[rows_k, :], MSB[...]
        a = jnp.where(core == 0, own, sib)
        b = jnp.where(core == 0, sib, own)
        master = jnp.where(low, a, swap(b))
        moment = jnp.where(low, swap(a), b)
        pseudo = master - mean
        moment_next = outer_momentum * moment + pseudo
        master_next = master - outer_rate * (pseudo + outer_momentum * moment_next)
        MW[rows_k, block_c] = master_next.astype(bf16)
        o_back_y.start()
        pack_0 = jnp.where(low, master_next, swap(moment_next))
        pack_1 = jnp.where(low, swap(master_next), moment_next)
        R1[...] = jnp.where(core == 0, pack_1, pack_0)
        o_pack.start()
        keep = jnp.where(core == 0, pack_0, pack_1)
        MN[rows_k, :] = keep[:, 0:64]
        MO[rows_k, :] = keep[:, 64:128]

    def outer_5():
        o_back_y_in.wait_recv()
        for j in range(3):
            o_back_x(j).start()
        o_pack.wait_recv()
        MN[rows_o, :] = R2[:, 0:64]
        MO[rows_o, :] = R2[:, 64:128]
        st_mn.start()
        st_mo.start()

    def outer_6():
        for j in range(3):
            o_back_x_in(j).wait_recv()
        o_back_s.start()

    def outer_7():
        o_back_s_in.wait_recv()
        FN[...] = (mixing * F[...].astype(f32) + (1.0 - mixing) * MW[...].astype(f32)).astype(bf16)
        st_fn.start()

    st_mn = pltpu.make_async_copy(MN, mn_out, l_s.at[8])
    st_mo = pltpu.make_async_copy(MO, mo_out, l_s.at[9])
    st_fn = pltpu.make_async_copy(FN, fn_out.at[0], l_s.at[10])

    def tables():
        doc_row = doc_ref[...].astype(f32)
        doc = column(doc_row)
        doc2 = jnp.concatenate([doc, doc], axis=1)
        row = jnp.broadcast_to(doc_row, (TOK, TOK))
        before = jnp.sum(jnp.where(row < doc2, 1.0, 0.0), axis=1, keepdims=True)
        token = lax.broadcasted_iota(jnp.int32, (TOK, HD), 0).astype(f32)
        position = token - before
        i = lax.broadcasted_iota(jnp.int32, (TOK, HD), 1)
        half = jnp.where(i < 64, i, i - 64).astype(f32)
        angle = position * jnp.exp(half * (-2.0 / HD * math.log(rope_base)))
        COS[...] = jnp.cos(angle)
        SIN[...] = jnp.where(i < 64, -1.0, 1.0) * jnp.sin(angle)
        u = lax.broadcasted_iota(jnp.int32, (TOK, TOK), 0)
        t = lax.broadcasted_iota(jnp.int32, (TOK, TOK), 1)
        bias = jnp.where((u <= t) & (row == doc2), 0.0, masked_score)
        BLO[...] = jnp.concatenate([bias[0:128, 0:128], bias[0:128, 0:128]], axis=1)
        BHI[...] = jnp.concatenate([bias[:, 128:256], bias[:, 128:256]], axis=1)

    def inverse():
        ld_x.wait()
        ld_xo.wait()
        a = X[0:TOK, :].astype(f32)
        total = jnp.sum(a * a, axis=1, keepdims=True)
        b = XO[...].astype(f32)
        total = total + jnp.sum(b * b, axis=1, keepdims=True)
        INV[...] = jnp.broadcast_to(lax.rsqrt(total * (1.0 / WIDE) + epsilon), (TOK, HD))
        CO[...] = jnp.zeros_like(CO)

    def transpose_x(who, j):
        XT[j * PIECE : (j + 1) * PIECE, who * TOK : (who + 1) * TOK] = X[
            who * TOK : (who + 1) * TOK, j * PIECE : (j + 1) * PIECE
        ].T

    def p_copy(g):
        return remote(POUT.at[g], PIN.at[g], p_s.at[g], p_r.at[g], partner)

    def project(g):
        POUT[g] = dot(X[TOK : 2 * TOK, :], WB[g]).astype(bf16)
        p_copy(g).start()
        PRAW[g] = dot(X[0:TOK, :], WB[g])

    def e_copy(g):
        return remote(E.at[g, 0:TOK], E.at[g, TOK : 2 * TOK], e_s.at[g], e_r.at[g], partner)

    def group_start(g):
        p_copy(g).wait_recv()
        raw = PRAW[g] + PIN[g].astype(f32)
        PRAW[g] = raw
        inv = INV[...]
        k = raw[:, 0:HD] * inv
        k = k * COS[...] + pltpu.roll(k, 64, 1) * SIN[...]
        kb = k.astype(bf16)
        KB[...] = kb
        KT[...] = kb.T
        VB[...] = (raw[:, HD : 2 * HD] * inv).astype(bf16)
        DKA[...] = jnp.zeros_like(DKA)
        DVA[...] = jnp.zeros_like(DVA)

    def group_end(g):
        dk = DKA[...] * SCALE
        inv = INV[...]
        dk = dk * COS[...] - pltpu.roll(dk, 64, 1) * SIN[...]
        ek = (dk * inv).astype(bf16)
        ev = (DVA[...] * inv).astype(bf16)
        E[g, 0:TOK, 0:HD] = ek
        E[g, 0:TOK, HD : 2 * HD] = ev
        e_copy(g).start()
        raw = PRAW[g]
        part = ek.astype(f32) * raw[:, 0:HD] + ev.astype(f32) * raw[:, HD : 2 * HD]
        CO[...] += jnp.broadcast_to(jnp.sum(part, axis=1, keepdims=True), (TOK, HD))

    def attend(kb, vb, kt, qc, dc, bias):
        s = dot_nt(kb, qc) + bias
        w = dot_nt(vb, dc)
        top = jnp.max(s, axis=0, keepdims=True)
        e = jnp.exp2((s - top) * EXP2_SCALE)
        p = e * (1.0 / jnp.sum(e, axis=0, keepdims=True))
        pw = p * w
        delta = jnp.sum(pw, axis=0, keepdims=True)
        ds = (pw - p * delta).astype(bf16)
        dq = (dot(kt, ds) * SCALE).T.astype(bf16)
        return dq, dot(ds, qc), dot(p.astype(bf16), dc)

    def head_pair(column_start):
        ca = pl.ds(al(column_start, 256), HD)
        cb = pl.ds(al(column_start + HD, HD), HD)
        low_rows, high_rows = slice(0, 128), slice(128, 256)

        def both(ref, rows):
            return jnp.concatenate([ref[rows, ca], ref[rows, cb]], axis=0)

        dq, dk, dv = attend(
            KB[...], VB[...], KT[...], both(Q, high_rows), both(DO, high_rows), BHI[...]
        )
        Q[high_rows, ca] = dq[0:128]
        Q[high_rows, cb] = dq[128:256]
        DKA[...] += dk
        DVA[...] += dv
        dq, dk, dv = attend(
            KB[low_rows, :], VB[low_rows, :], KT[:, low_rows],
            both(Q, low_rows), both(DO, low_rows), BLO[...],
        )
        Q[low_rows, ca] = dq[0:128]
        Q[low_rows, cb] = dq[128:256]
        DKA[low_rows, :] += dk
        DVA[low_rows, :] += dv

    def dq_store(g):
        cols = pl.ds(al(g * 1024, 1024), 1024)
        return pltpu.make_async_copy(Q.at[:, cols], dq_out.at[:, cols], l_s.at[11 + g])

    def rs_copy(d, g, s):
        i = ag_sem(d, g, s)
        if s == 1:
            rows = slice(d * 128, d * 128 + 128)
            src, dst = SB.at[i, rows], RB.at[i, rows]
        else:
            src, dst = SB.at[i], RB.at[i]
        return remote(src, dst, rs_s.at[i], rs_r.at[i], (right, left)[d])

    def term(owner, g):
        return dot(XT[pl.ds(al(owner * TOK, TOK), TOK), :], E[g])

    def rs_step(g, s):
        for d in (0, 1):
            owner = ring_at(5 - s if d == 0 else s - 5)
            i = ag_sem(d, g, s)
            if s == 1:
                start = al(owner * TOK + d * 128, 128)
                SB[i, d * 128 : d * 128 + 128] = dot(XT[pl.ds(start, 128), :], E[g]).astype(bf16)
            else:
                total = term(owner, g)
                rs_copy(d, g, s - 1).wait_recv()
                if s == 2:
                    came = slice(d * 128, d * 128 + 128)
                    rest = slice((1 - d) * 128, (1 - d) * 128 + 128)
                    SB[i, came] = (total[came] + RB[i - 1, came].astype(f32)).astype(bf16)
                    SB[i, rest] = total[rest].astype(bf16)
                else:
                    SB[i] = (total + RB[i - 1].astype(f32)).astype(bf16)
            rs_copy(d, g, s).start()

    def rs_end(g):
        total = term(z, g)
        for d in (0, 1):
            rs_copy(d, g, 4).wait_recv()
            total = total + RB[ag_sem(d, g, 4)].astype(f32)
        ck, cv = g * HD, 512 + g * HD
        wide_gain = GC[...]
        tk, tv = total[:, 0:HD], total[:, HD : 2 * HD]
        DW[:, ck : ck + HD] = tk * wide_gain
        DW[:, cv : cv + HD] = tv * wide_gain
        part = tk * WR[:, ck : ck + HD].astype(f32) + tv * WR[:, cv : cv + HD].astype(f32)
        return jnp.sum(part, axis=1, keepdims=True)

    def u_copy(j):
        return remote(UOUT.at[j], UIN.at[j], u_s.at[j], u_r.at[j], partner)

    def upstream(first, j):
        rows = slice(j * PIECE, (j + 1) * PIECE)
        total = dot_nt(E[0, first : first + TOK], WB[0, rows])
        for g in range(1, GROUPS):
            total = total + dot_nt(E[g, first : first + TOK], WB[g, rows])
        return total

    def dx_store(part, j):
        start = al((h if part == 0 else 1 - h) * HALF + j * PIECE, PIECE)
        return pltpu.make_async_copy(
            DX.at[part * PIECES + j], dx_out.at[:, pl.ds(start, PIECE)], l_s.at[15 + part * PIECES + j]
        )

    def send_upstream(j):
        UOUT[j] = upstream(TOK, j).astype(bf16)
        u_copy(j).start()

    def finish(part, j, u):
        cols = slice(j * PIECE, (j + 1) * PIECE)
        x = X[0:TOK, cols] if part == 0 else XO[:, cols]
        c = CO[...]
        c = jnp.concatenate([c] * (PIECE // HD), axis=1)
        DX[part * PIECES + j] = (u - x.astype(f32) * c).astype(bf16)
        dx_store(part, j).start()

    outer_1()
    tables()
    ag_step(0, 1)
    outer_2()
    ag_step(1, 1)
    inverse()
    ag_step(0, 2)
    transpose_x(0, 0)
    transpose_x(0, 1)
    ag_step(1, 2)
    transpose_x(0, 2)
    transpose_x(0, 3)
    outer_3()
    ag_step(0, 3)
    x_copy(0).wait_recv()
    transpose_x(1, 0)
    ag_step(1, 3)
    for g in (2, 3):
        for d in (0, 1):
            ag_send(d, g, 1).start()
    outer_4()
    x_copy(1).wait_recv()
    transpose_x(1, 1)
    ag_step(0, 4)
    ag_step(1, 4)
    outer_5()
    x_copy(2).wait_recv()
    transpose_x(1, 2)
    x_copy(3).wait_recv()
    project(0)
    project(1)
    transpose_x(1, 3)
    ld_q.wait()
    ld_do.wait()

    def attention(base, hook):
        def step(n, _):
            g = base + lax.div(n, PAIRS)
            part = lax.rem(n, PAIRS)

            @pl.when(part == 0)
            def _():
                group_start(g)

            head_pair((base * PAIRS + n) * 2 * HD)

            @pl.when(part == PAIRS - 1)
            def _():
                group_end(g)
                dq_store(g).start()

            hook(n)
            return 0

        lax.fori_loop(0, 2 * PAIRS, step, 0)

    def ag_hook(n):
        g, hop = 2 + lax.rem(n, 2), lax.div(n, 2)
        for s in (1, 2, 3, 4):

            @pl.when(hop == s - 1)
            def _(s=s):
                ag_step(g, s)

    def rs_hook(n):
        g, hop = lax.rem(n, 2), lax.div(n, 2)
        for s in (1, 2, 3, 4):

            @pl.when(hop == s - 1)
            def _(s=s):
                rs_step(g, s)

    attention(0, ag_hook)
    outer_6()
    project(2)
    project(3)
    for g in (0, 1):
        e_copy(g).wait_recv()
    attention(2, rs_hook)
    outer_7()
    e_copy(2).wait_recv()
    rs_step(2, 1)
    e_copy(3).wait_recv()
    rs_step(3, 1)
    CO[...] = CO[...] * INV[...] * INV[...] * (1.0 / WIDE)
    for j in range(PIECES):
        send_upstream(j)
    rs_step(2, 2)
    rs_step(3, 2)
    gain_total = rs_end(0)
    finish(0, 0, upstream(0, 0))
    rs_step(2, 3)
    rs_step(3, 3)
    gain_total = gain_total + rs_end(1)
    finish(0, 1, upstream(0, 1))
    rs_step(2, 4)
    rs_step(3, 4)
    finish(0, 2, upstream(0, 2))
    finish(0, 3, upstream(0, 3))
    for j in range(PIECES - 1):
        u_copy(j).wait_recv()
        finish(1, j, UIN[j].astype(f32))
    gain_total = gain_total + rs_end(2)
    gain_total = gain_total + rs_end(3)
    st_dw = pltpu.make_async_copy(DW, dw_out.at[0], l_s.at[23])
    st_dw.start()
    spread = jnp.where(eye, jnp.broadcast_to(gain_total, (TOK, TOK)), 0.0)
    DG[...] = jnp.sum(spread, axis=0, keepdims=True)
    st_dg = pltpu.make_async_copy(DG, dg_out, l_s.at[24])
    st_dg.start()
    u_copy(PIECES - 1).wait_recv()
    finish(1, PIECES - 1, UIN[PIECES - 1].astype(f32))

    for j in range(PIECES):
        x_copy(j).wait_send()
        u_copy(j).wait_send()

    def drain(g, _):
        p_copy(g).wait_send()
        e_copy(g).wait_send()
        for s in (1, 2, 3, 4):
            for d in (0, 1):
                ag_send(d, g, s).wait_send()
                rs_copy(d, g, s).wait_send()
        dq_store(g).wait()
        return 0

    lax.fori_loop(0, GROUPS, drain, 0)
    for c in (o_frag, o_state, o_y, o_pack, o_back_y, o_back_s):
        c.wait_send()
    for j in range(3):
        o_x(j).wait_send()
        o_back_x(j).wait_send()
    for part in (0, 1):
        for j in range(PIECES):
            dx_store(part, j).wait()
    for c in (st_mn, st_mo, st_fn, st_dw, st_dg):
        c.wait()


def on_device(x, q, do, doc, gain, w, fl, fm, fmo):
    sds = jax.ShapeDtypeStruct
    hbm = pl.BlockSpec(memory_space=pl.ANY)
    vmem = pl.BlockSpec(memory_space=pltpu.VMEM)

    def v(shape, t):
        return pltpu.VMEM(shape, t)

    dma = pltpu.SemaphoreType.DMA
    scratch = [
        v((2 * TOK, HALF), bf16),
        v((TOK, HALF), bf16),
        v((HALF, 2 * TOK), bf16),
        v((TOK, WIDE), bf16),
        v((TOK, WIDE), bf16),
        v((TOK, 1024), bf16),
        v((GROUPS, HALF, 256), bf16),
        v((GROUPS, TOK, 256), bf16),
        v((GROUPS, TOK, 256), bf16),
        v((GROUPS, TOK, 256), f32),
        v((GROUPS, 2 * TOK, 256), bf16),
        v((PIECES, TOK, PIECE), bf16),
        v((PIECES, TOK, PIECE), bf16),
        v((2 * PIECES, TOK, PIECE), bf16),
        v((32, TOK, 256), bf16),
        v((32, TOK, 256), bf16),
        v((TOK, 1024), f32),
        v((TOK, HD), f32),
        v((TOK, HD), f32),
        v((TOK, HD), f32),
        v((TOK, HD), f32),
        v((128, 256), f32),
        v((256, 256), f32),
        v((TOK, HD), bf16),
        v((TOK, HD), bf16),
        v((HD, TOK), bf16),
        v((TOK, HD), f32),
        v((TOK, HD), f32),
        v((TOK, HD), f32),
        v((1, TOK), f32),
        v((256, 1024), bf16),
        v((128, 1024), bf16),
        v((128, 1024), bf16),
        v((3, 128, 256), bf16),
        v((128, 128), bf16),
        v((128, 128), bf16),
        v((256, 1024), bf16),
        v((256, 1024), bf16),
        v((256, 64), f32),
        v((256, 64), f32),
        v((256, 128), f32),
        v((128, 128), f32),
        v((128, 128), f32),
        v((128, 128), f32),
        v((256, 64), f32),
        v((256, 64), f32),
        dma((32,)), dma((32,)), dma((32,)), dma((32,)),
        dma((4,)), dma((4,)), dma((4,)), dma((4,)),
        dma((4,)), dma((4,)), dma((4,)), dma((4,)),
        dma((12,)), dma((12,)), dma((25,)),
    ]
    return pl.pallas_call(
        kernel,
        out_shape=(
            sds((TOK, WIDE), bf16),
            sds((TOK, WIDE), bf16),
            sds((1, 256, 1024), f32),
            sds((1, 256), f32),
            sds((256, 64), f32),
            sds((256, 64), f32),
            sds((1, 256, 1024), bf16),
        ),
        in_specs=[hbm, hbm, hbm, vmem, vmem, hbm, hbm, hbm, hbm],
        out_specs=(hbm,) * 7,
        scratch_shapes=scratch,
        compiler_params=pltpu.CompilerParams(
            collective_id=0, has_side_effects=True, vmem_limit_bytes=48 * 2**20
        ),
        name="step",
    )(x, q, do, doc, gain, w, fl, fm, fmo)


def solution(mesh):
    placed = (
        P(("rep", "fsdp"), None),
        P(("rep", "fsdp"), None),
        P(("rep", "fsdp"), None),
        P(("rep", "fsdp"), None),
        P("rep", "fsdp"),
        P("rep", "fsdp", None),
        P("rep", "fsdp", None),
        P("fsdp", "rep"),
        P("fsdp", "rep"),
    )
    return jax.shard_map(
        on_device,
        mesh=mesh,
        in_specs=placed,
        out_specs=(
            P(("rep", "fsdp"), None),
            P(("rep", "fsdp"), None),
            P("rep", "fsdp", None),
            P("rep", "fsdp"),
            P("fsdp", "rep"),
            P("fsdp", "rep"),
            P("rep", "fsdp", None),
        ),
        check_vma=False,
    )
```

```python
import math

import jax
import jax.numpy as jnp
from jax import lax
from jax.experimental import pallas as pl
from jax.experimental.pallas import tpu as pltpu
from jax.sharding import PartitionSpec as P

epsilon = 1e-05
rope_base = 500000.0
outer_rate = 0.7
outer_momentum = 0.9
mixing = 0.5
masked_score = -1e30

TOK = 256
WIDE = 4096
HALF = 2048
GROUPS = 4
PAIRS = 4
HD = 128
RING = 8
SCALE = HD ** (-0.5)
EXP2_SCALE = SCALE * math.log2(math.e)
PIECE = 512
PIECES = HALF // PIECE

f32 = jnp.float32
bf16 = jnp.bfloat16
VMEM_LIMIT = 40 * 2**20
NT = (((1,), (1,)), ((), ()))


BEFORE = (
    ("inv",), ("tab",), ("tr", 0, 0), ("tr", 0, 1), ("tr", 0, 2), ("tr", 0, 3), ("o", 1), ("o", 2),
    ("ag", 0, 0, 1), ("ag", 1, 0, 1), ("tr", 1, 0), ("ag", 0, 1, 1), ("ag", 1, 1, 1), ("ag", 0, 0, 2),
    ("ag", 1, 0, 2), ("own", 2), ("o", 3), ("tr", 1, 1), ("ag", 0, 1, 2), ("ag", 1, 1, 2),
    ("ag", 0, 0, 3), ("ag", 1, 0, 3), ("tr", 1, 2), ("ag", 0, 2, 1), ("ag", 1, 2, 1), ("own", 3),
    ("ag", 0, 1, 3), ("ag", 1, 1, 3), ("ag", 0, 0, 4), ("ag", 1, 0, 4), ("po", 0), ("pp", 0),
    ("tr", 1, 3), ("o", 4), ("ag", 0, 2, 2), ("ag", 1, 2, 2), ("ag", 0, 3, 1), ("ag", 1, 3, 1),
    ("gs", 0),
)
DURING = (
    (),
    (
        ("ag", 0, 1, 4), ("ag", 1, 1, 4), ("pp", 1), ("po", 1),
    ),
    (),
    (
        ("ag", 0, 2, 3), ("ag", 1, 2, 3),
    ),
    (
        ("ge", 0), ("o", 5), ("gs", 1),
    ),
    (
        ("ag", 0, 3, 2), ("ag", 1, 3, 2),
    ),
    (
        ("ag", 0, 2, 4), ("ag", 1, 2, 4), ("pp", 2), ("po", 2),
    ),
    (
        ("ew", 0), ("rs", 0, 0, 1), ("rs", 1, 0, 1),
    ),
    (
        ("ge", 1), ("ag", 0, 3, 3), ("ag", 1, 3, 3), ("o", 6), ("gs", 2), ("rs", 0, 0, 2), ("rs", 1, 0, 2),
    ),
    (
        ("ag", 0, 3, 4), ("ag", 1, 3, 4), ("pp", 3), ("po", 3),
    ),
    (
        ("ew", 1), ("rs", 0, 1, 1), ("rs", 1, 1, 1),
    ),
    (
        ("rs", 0, 0, 3), ("rs", 1, 0, 3),
    ),
    (
        ("ge", 2), ("gs", 3), ("rs", 0, 1, 2), ("rs", 1, 1, 2),
    ),
    (),
    (),
    (
        ("rs", 0, 0, 4), ("rs", 1, 0, 4),
    ),
)
AFTER = (
    ("ew", 2), ("ge", 3), ("rs", 0, 1, 3), ("rs", 1, 1, 3), ("rs", 0, 2, 1), ("rs", 1, 2, 1),
    ("uo", 0), ("uo", 1), ("uo", 2), ("uo", 3), ("o", 7), ("re", 0), ("ew", 3), ("us", 0),
    ("rs", 0, 3, 1), ("rs", 1, 3, 1), ("us", 1), ("us", 2), ("us", 3), ("rs", 0, 1, 4),
    ("rs", 1, 1, 4), ("rs", 0, 2, 2), ("rs", 1, 2, 2), ("rs", 0, 3, 2), ("rs", 1, 3, 2), ("re", 1),
    ("ui", 0), ("rs", 0, 2, 3), ("rs", 1, 2, 3), ("rs", 0, 3, 3), ("rs", 1, 3, 3), ("ui", 1),
    ("rs", 0, 2, 4), ("rs", 1, 2, 4), ("rs", 0, 3, 4), ("rs", 1, 3, 4), ("ui", 2), ("re", 2),
    ("re", 3), ("ui", 3),
)


def dot(a, b):
    return jnp.dot(a, b, preferred_element_type=f32)


def dot_nt(a, b):
    return lax.dot_general(a, b, NT, preferred_element_type=f32)


def kernel(
    x_ref, q_ref, do_ref, doc_ref, gain_ref, w_ref, fl_ref, fm_ref, fmo_ref,
    dq_out, dx_out, dw_out, dg_out, mn_out, mo_out, fn_out,
    X, XO, XT, Q, DO, WR, WB, PIN, POUT, PRAW, E, UOUT, UIN, RB, SB,
    INV, CO, COS, SIN, BLO, BHI, KB, VB, KT, DKA, DVA, GC, GT,
    F, FS, FSUM, XR, YS, YR, MW, M01, MB, MSB, R1, R2, PK, DOC, GAIN,
    ag_s, ag_r, rs_s, rs_r, x_s, x_r, p_s, p_r, e_s, e_r, u_s, u_r, o_s, o_r, l_s,
):
    f = lax.axis_index("fsdp")
    r = lax.axis_index("rep")
    z = lax.rem(f, RING)
    h = lax.div(f, RING)
    core = lax.rem(r, 2)
    yh = lax.rem(lax.div(r, 2), 2)
    xx = lax.div(r, 4)

    right = {"fsdp": h * RING + lax.rem(z + 1, RING)}
    left = {"fsdp": h * RING + lax.rem(z + RING - 1, RING)}
    partner = {"fsdp": (1 - h) * RING + z}
    sibling = {"rep": xx * 4 + yh * 2 + (1 - core)}
    across = {"rep": xx * 4 + (1 - yh) * 2 + core}
    xpeer = [{"rep": lax.rem(xx + j, 4) * 4 + yh * 2 + core} for j in (1, 2, 3)]

    def remote(src, dst, ssem, rsem, device):
        return pltpu.make_async_remote_copy(
            src_ref=src, dst_ref=dst, send_sem=ssem, recv_sem=rsem,
            device_id=device, device_id_type=pl.DeviceIdType.MESH,
        )

    def al(value, m):
        return pl.multiple_of(value, m)

    mine = pl.ds(al(h * HALF, HALF), HALF)
    other = pl.ds(al((1 - h) * HALF, HALF), HALF)
    ld_w = pltpu.make_async_copy(w_ref.at[0], WR, l_s.at[0])
    ld_x = pltpu.make_async_copy(x_ref.at[:, mine], X.at[0:TOK], l_s.at[1])
    ld_xo = pltpu.make_async_copy(x_ref.at[:, other], XO, l_s.at[2])
    ld_q = pltpu.make_async_copy(q_ref, Q, l_s.at[3])
    ld_do = pltpu.make_async_copy(do_ref, DO, l_s.at[4])
    ld_f = pltpu.make_async_copy(fl_ref.at[0], F, l_s.at[5])
    ld_m0 = pltpu.make_async_copy(fm_ref, M01.at[0:64], l_s.at[6])
    ld_m1 = pltpu.make_async_copy(fmo_ref, M01.at[64:128], l_s.at[7])
    ld_doc = pltpu.make_async_copy(doc_ref, DOC, l_s.at[8])
    ld_gain = pltpu.make_async_copy(gain_ref, GAIN, l_s.at[9])
    for c in (ld_w, ld_gain, ld_x, ld_xo, ld_f, ld_m0, ld_m1, ld_doc, ld_q, ld_do):
        c.start()

    barrier = pltpu.get_barrier_semaphore()
    for d in (left, right, partner, sibling, across, *xpeer):
        pl.semaphore_signal(barrier, inc=1, device_id=d, device_id_type=pl.DeviceIdType.MESH)

    def x_copy(j):
        return remote(
            x_ref.at[:, pl.ds(al((1 - h) * HALF + j * PIECE, PIECE), PIECE)],
            X.at[TOK : 2 * TOK, j * PIECE : (j + 1) * PIECE],
            x_s.at[j], x_r.at[j], partner,
        )

    def ring_at(dist):
        return lax.rem(z + dist + 2 * RING, RING)

    def ag_sem(d, g, s):
        return d * 16 + g * 4 + (s - 1)

    def ag_copy(d, g, s, shard):
        start, size = (shard * TOK, TOK) if s < 4 else (shard * TOK + d * 128, 128)
        block = WB.at[g, pl.ds(al(start, 128), size)]
        i = ag_sem(d, g, s)
        return remote(block, block, ag_s.at[i], ag_r.at[i], (right, left)[d])

    def ag_send(d, g, s):
        return ag_copy(d, g, s, ring_at((1 - s) if d == 0 else (s - 1)))

    def ag_recv(d, g, s):
        return ag_copy(d, g, s, ring_at(-s if d == 0 else s))

    def ag_step(d, g, s):
        ag_recv(d, g, s).wait_recv()
        if s < 4:
            ag_send(d, g, s + 1).start()

    def ag_own(g):
        for d in (0, 1):
            ag_send(d, g, 1).start()

    eye = lax.broadcasted_iota(jnp.int32, (TOK, TOK), 0) == lax.broadcasted_iota(jnp.int32, (TOK, TOK), 1)

    def column(row):
        square = jnp.where(eye, jnp.broadcast_to(row, (TOK, TOK)), 0.0).astype(bf16)
        return dot(square, jnp.ones((TOK, HD), bf16))

    ld_gain.wait()
    gain_row = GAIN[...].astype(f32)
    gain = column(gain_row)
    GC[...] = gain
    ld_w.wait()
    own_rows = pl.ds(al(z * TOK, TOK), TOK)

    def scale_w(g):
        WB[g, own_rows, 0:HD] = (WR[:, g * HD : (g + 1) * HD].astype(f32) * gain).astype(bf16)
        WB[g, own_rows, HD : 2 * HD] = (
            WR[:, 512 + g * HD : 512 + (g + 1) * HD].astype(f32) * gain
        ).astype(bf16)

    scale_w(0)
    pl.semaphore_wait(barrier, 8)
    x_copy(0).start()
    ag_own(0)
    for j in range(1, PIECES):
        x_copy(j).start()
    scale_w(1)
    ag_own(1)
    scale_w(2)
    scale_w(3)

    rows_k = pl.ds(al(core * 128, 128), 128)
    rows_o = pl.ds(al((1 - core) * 128, 128), 128)
    lane = lax.broadcasted_iota(jnp.int32, (128, 128), 1)
    low = lane < 64
    block_c = pl.ds(al((2 * xx + yh) * 128, 128), 128)
    block_x = pl.ds(al(xx * 256, 256), 256)

    def swap(v):
        return pltpu.roll(v, 64, 1)

    o_frag = remote(F.at[rows_o], FS, o_s.at[0], o_r.at[0], sibling)
    o_state = remote(MB.at[rows_o], MSB, o_s.at[1], o_r.at[1], sibling)

    def o_x(j):
        to = lax.rem(xx + j + 1, 4)
        return remote(
            FSUM.at[:, pl.ds(al(to * 256, 256), 256)], XR.at[j], o_s.at[2 + j], o_r.at[2 + j], xpeer[j]
        )

    o_y = remote(YS, YR, o_s.at[5], o_r.at[5], across)
    o_pack = remote(R1, R2, o_s.at[6], o_r.at[6], sibling)

    def mw(rows, cols, i, device):
        return remote(MW.at[rows, cols], MW.at[rows, cols], o_s.at[i], o_r.at[i], device)

    o_back_y = mw(rows_k, block_c, 7, across)
    block_c_across = pl.ds(al((2 * xx + 1 - yh) * 128, 128), 128)
    o_back_y_in = mw(rows_k, block_c_across, 7, across)

    def o_back_x(j):
        return mw(rows_k, block_x, 8 + j, xpeer[j])

    def o_back_x_in(j):
        frm = lax.rem(xx + 4 - (j + 1), 4)
        return mw(rows_k, pl.ds(al(frm * 256, 256), 256), 8 + j, xpeer[j])

    o_back_s = mw(rows_k, slice(None), 11, sibling)
    o_back_s_in = mw(rows_o, slice(None), 11, sibling)

    def outer_1():
        ld_f.wait()
        ld_m0.wait()
        ld_m1.wait()
        MB[...] = M01[...].T
        o_frag.start()
        o_state.start()

    def outer_2():
        o_frag.wait_recv()
        FSUM[...] = (F[rows_k, :].astype(f32) + FS[...].astype(f32)).astype(bf16)
        for j in range(3):
            o_x(j).start()

    def outer_3():
        for j in range(3):
            o_x(j).wait_recv()
        total = FSUM[:, block_x].astype(f32)
        for j in range(3):
            total = total + XR[j].astype(f32)
        first, second = total[:, 0:128], total[:, 128:256]
        YS[...] = jnp.where(yh == 0, second, first).astype(bf16)
        R1[...] = jnp.where(yh == 0, first, second)
        o_y.start()

    def outer_4():
        o_y.wait_recv()
        o_state.wait_recv()
        mean = (R1[...] + YR[...].astype(f32)) * (1.0 / 16.0)
        own, sib = MB[rows_k, :], MSB[...]
        a = jnp.where(core == 0, own, sib)
        b = jnp.where(core == 0, sib, own)
        master = jnp.where(low, a, swap(b))
        moment = jnp.where(low, swap(a), b)
        pseudo = master - mean
        moment_next = outer_momentum * moment + pseudo
        master_next = master - outer_rate * (pseudo + outer_momentum * moment_next)
        MW[rows_k, block_c] = master_next.astype(bf16)
        o_back_y.start()
        pack_0 = jnp.where(low, master_next, swap(moment_next))
        pack_1 = jnp.where(low, swap(master_next), moment_next)
        R1[...] = jnp.where(core == 0, pack_1, pack_0)
        o_pack.start()
        keep = jnp.where(core == 0, pack_0, pack_1)
        PK[rows_k, :] = keep

    def outer_5():
        o_back_y_in.wait_recv()
        for j in range(3):
            o_back_x(j).start()
        o_pack.wait_recv()
        PK[rows_o, :] = R2[...]
        both = PK[...].T
        mn_out[...] = both[0:64]
        mo_out[...] = both[64:128]

    def outer_6():
        for j in range(3):
            o_back_x_in(j).wait_recv()
        o_back_s.start()

    def outer_7():
        o_back_s_in.wait_recv()
        fn_out[0] = (mixing * F[...].astype(f32) + (1.0 - mixing) * MW[...].astype(f32)).astype(bf16)

    def tables():
        ld_doc.wait()
        doc_row = DOC[...].astype(f32)
        doc = column(doc_row)
        doc2 = jnp.concatenate([doc, doc], axis=1)
        row = jnp.broadcast_to(doc_row, (TOK, TOK))
        before = jnp.sum(jnp.where(row < doc2, 1.0, 0.0), axis=1, keepdims=True)
        token = lax.broadcasted_iota(jnp.int32, (TOK, HD), 0).astype(f32)
        position = token - before
        i = lax.broadcasted_iota(jnp.int32, (TOK, HD), 1)
        half = jnp.where(i < 64, i, i - 64).astype(f32)
        angle = position * jnp.exp(half * (-2.0 / HD * math.log(rope_base)))
        COS[...] = jnp.cos(angle)
        SIN[...] = jnp.where(i < 64, -1.0, 1.0) * jnp.sin(angle)
        u = lax.broadcasted_iota(jnp.int32, (TOK, TOK), 0)
        t = lax.broadcasted_iota(jnp.int32, (TOK, TOK), 1)
        bias = jnp.where((u <= t) & (row == doc2), 0.0, masked_score)
        BLO[...] = jnp.concatenate([bias[0:128, 0:128], bias[0:128, 0:128]], axis=1)
        BHI[...] = jnp.concatenate([bias[:, 128:256], bias[:, 128:256]], axis=1)

    def inverse():
        ld_x.wait()
        ld_xo.wait()
        a = X[0:TOK, :].astype(f32)
        total = jnp.sum(a * a, axis=1, keepdims=True)
        b = XO[...].astype(f32)
        total = total + jnp.sum(b * b, axis=1, keepdims=True)
        INV[...] = jnp.broadcast_to(lax.rsqrt(total * (1.0 / WIDE) + epsilon), (TOK, HD))
        CO[...] = jnp.zeros_like(CO)

    def transpose_x(who, j):
        XT[j * PIECE : (j + 1) * PIECE, who * TOK : (who + 1) * TOK] = X[
            who * TOK : (who + 1) * TOK, j * PIECE : (j + 1) * PIECE
        ].T

    def p_copy(g):
        return remote(POUT.at[g], PIN.at[g], p_s.at[g], p_r.at[g], partner)

    def project_partner(g):
        POUT[g] = dot(X[TOK : 2 * TOK, :], WB[g]).astype(bf16)
        p_copy(g).start()

    def project_own(g):
        PRAW[g] = dot(X[0:TOK, :], WB[g])

    def e_copy(g):
        return remote(E.at[g, 0:TOK], E.at[g, TOK : 2 * TOK], e_s.at[g], e_r.at[g], partner)

    def group_start(g):
        p_copy(g).wait_recv()
        raw = PRAW[g] + PIN[g].astype(f32)
        PRAW[g] = raw
        inv = INV[...]
        k = raw[:, 0:HD] * inv
        k = k * COS[...] + pltpu.roll(k, 64, 1) * SIN[...]
        kb = k.astype(bf16)
        KB[...] = kb
        KT[...] = kb.T
        VB[...] = (raw[:, HD : 2 * HD] * inv).astype(bf16)
        DKA[...] = jnp.zeros_like(DKA)
        DVA[...] = jnp.zeros_like(DVA)

    def group_end(g):
        dk = DKA[...] * SCALE
        inv = INV[...]
        dk = dk * COS[...] - pltpu.roll(dk, 64, 1) * SIN[...]
        ek = (dk * inv).astype(bf16)
        ev = (DVA[...] * inv).astype(bf16)
        E[g, 0:TOK, 0:HD] = ek
        E[g, 0:TOK, HD : 2 * HD] = ev
        e_copy(g).start()
        raw = PRAW[g]
        part = ek.astype(f32) * raw[:, 0:HD] + ev.astype(f32) * raw[:, HD : 2 * HD]
        CO[...] += jnp.broadcast_to(jnp.sum(part, axis=1, keepdims=True), (TOK, HD))

    def attend(kb, vb, kt, qc, dc, bias):
        s = dot_nt(kb, qc) + bias
        w = dot_nt(vb, dc)
        top = jnp.max(s, axis=0, keepdims=True)
        e = jnp.exp2((s - top) * EXP2_SCALE)
        p = e * (1.0 / jnp.sum(e, axis=0, keepdims=True))
        pw = p * w
        delta = jnp.sum(pw, axis=0, keepdims=True)
        ds = (pw - p * delta).astype(bf16)
        dq = (dot(kt, ds) * SCALE).T.astype(bf16)
        return dq, dot(ds, qc), dot(p.astype(bf16), dc)

    def head_pair(column_start):
        ca = pl.ds(al(column_start, 256), HD)
        cb = pl.ds(al(column_start + HD, HD), HD)
        low_rows, high_rows = slice(0, 128), slice(128, 256)

        def both(ref, rows):
            return jnp.concatenate([ref[rows, ca], ref[rows, cb]], axis=0)

        dq, dk, dv = attend(
            KB[...], VB[...], KT[...], both(Q, high_rows), both(DO, high_rows), BHI[...]
        )
        dq_out[high_rows, ca] = dq[0:128]
        dq_out[high_rows, cb] = dq[128:256]
        DKA[...] += dk
        DVA[...] += dv
        dq, dk, dv = attend(
            KB[low_rows, :], VB[low_rows, :], KT[:, low_rows],
            both(Q, low_rows), both(DO, low_rows), BLO[...],
        )
        dq_out[low_rows, ca] = dq[0:128]
        dq_out[low_rows, cb] = dq[128:256]
        DKA[low_rows, :] += dk
        DVA[low_rows, :] += dv

    def rs_copy(d, g, s):
        i = ag_sem(d, g, s)
        if s == 1:
            rows = slice(d * 128, d * 128 + 128)
            src, dst = SB.at[i, rows], RB.at[i, rows]
        else:
            src, dst = SB.at[i], RB.at[i]
        return remote(src, dst, rs_s.at[i], rs_r.at[i], (right, left)[d])

    def term(owner, g):
        return dot(XT[pl.ds(al(owner * TOK, TOK), TOK), :], E[g])

    def rs_step(d, g, s):
        owner = ring_at(5 - s if d == 0 else s - 5)
        i = ag_sem(d, g, s)
        if s == 1:
            start = al(owner * TOK + d * 128, 128)
            SB[i, d * 128 : d * 128 + 128] = dot(XT[pl.ds(start, 128), :], E[g]).astype(bf16)
        else:
            total = term(owner, g)
            rs_copy(d, g, s - 1).wait_recv()
            if s == 2:
                came = slice(d * 128, d * 128 + 128)
                rest = slice((1 - d) * 128, (1 - d) * 128 + 128)
                SB[i, came] = (total[came] + RB[i - 1, came].astype(f32)).astype(bf16)
                SB[i, rest] = total[rest].astype(bf16)
            else:
                SB[i] = (total + RB[i - 1].astype(f32)).astype(bf16)
        rs_copy(d, g, s).start()

    def rs_end(g):
        total = term(z, g)
        for d in (0, 1):
            rs_copy(d, g, 4).wait_recv()
            total = total + RB[ag_sem(d, g, 4)].astype(f32)
        ck, cv = g * HD, 512 + g * HD
        wide_gain = GC[...]
        tk, tv = total[:, 0:HD], total[:, HD : 2 * HD]
        dw_out[0, :, ck : ck + HD] = tk * wide_gain
        dw_out[0, :, cv : cv + HD] = tv * wide_gain
        part = tk * WR[:, ck : ck + HD].astype(f32) + tv * WR[:, cv : cv + HD].astype(f32)
        GT[...] += jnp.broadcast_to(jnp.sum(part, axis=1, keepdims=True), (TOK, HD))

    def u_copy(j):
        return remote(UOUT.at[j], UIN.at[j], u_s.at[j], u_r.at[j], partner)

    def upstream(first, j):
        rows = slice(j * PIECE, (j + 1) * PIECE)
        total = dot_nt(E[0, first : first + TOK], WB[0, rows])
        for g in range(1, GROUPS):
            total = total + dot_nt(E[g, first : first + TOK], WB[g, rows])
        return total

    def send_upstream(j):
        UOUT[j] = upstream(TOK, j).astype(bf16)
        u_copy(j).start()

    def finish(part, j, u):
        cols = slice(j * PIECE, (j + 1) * PIECE)
        x = X[0:TOK, cols] if part == 0 else XO[:, cols]
        c = CO[...]
        c = jnp.concatenate([c] * (PIECE // HD), axis=1)
        start = al((h if part == 0 else 1 - h) * HALF + j * PIECE, PIECE)
        dx_out[:, pl.ds(start, PIECE)] = (u - x.astype(f32) * c).astype(bf16)

    def outer(k):
        (outer_1, outer_2, outer_3, outer_4, outer_5, outer_6, outer_7)[k - 1]()

    def x_transpose(who, j):
        if who == 1 and j < PIECES - 1:
            x_copy(j).wait_recv()
        transpose_x(who, j)

    def start_group(g):
        if g == 0:
            ld_q.wait()
            ld_do.wait()
        group_start(g)

    def end_group(g):
        group_end(g)
        if g == GROUPS - 1:
            CO[...] = CO[...] * INV[...] * INV[...] * (1.0 / WIDE)

    def first_projection(g):
        if g == 0:
            x_copy(PIECES - 1).wait_recv()
        project_partner(g)

    def upstream_in(j):
        u_copy(j).wait_recv()
        finish(1, j, UIN[j].astype(f32))

    acts = dict(
        ag=ag_step, own=ag_own, tab=tables, inv=inverse, tr=x_transpose, pp=first_projection, po=project_own,
        gs=start_group, ge=end_group, rs=rs_step, ew=lambda g: e_copy(g).wait_recv(), re=rs_end, us=send_upstream,
        uo=lambda j: finish(0, j, upstream(0, j)), ui=upstream_in, o=outer,
    )

    def play(items):
        for name, *numbers in items:
            acts[name](*numbers)

    GT[...] = jnp.zeros_like(GT)
    play(BEFORE)

    def step(n, _):
        for k, items in enumerate(DURING):
            if items:

                @pl.when(n == k)
                def _(items=items):
                    play(items)

        head_pair(n * 2 * HD)
        return 0

    lax.fori_loop(0, GROUPS * PAIRS, step, 0)
    play(AFTER)
    spread = jnp.where(eye, jnp.concatenate([GT[...], GT[...]], axis=1), 0.0)
    dg_out[...] = jnp.sum(spread, axis=0, keepdims=True)

    for j in range(PIECES):
        x_copy(j).wait_send()
        u_copy(j).wait_send()

    def drain(g, _):
        p_copy(g).wait_send()
        e_copy(g).wait_send()
        for s in (1, 2, 3, 4):
            for d in (0, 1):
                ag_send(d, g, s).wait_send()
                rs_copy(d, g, s).wait_send()
        return 0

    lax.fori_loop(0, GROUPS, drain, 0)
    for c in (o_frag, o_state, o_y, o_pack, o_back_y, o_back_s):
        c.wait_send()
    for j in range(3):
        o_x(j).wait_send()
        o_back_x(j).wait_send()


def store(*refs):
    n = len(refs) // 2
    sems = refs[-1]
    copies = [pltpu.make_async_copy(refs[i], refs[n + i], sems.at[i]) for i in range(n)]
    for c in copies:
        c.start()
    for c in copies:
        c.wait()


def on_device(x, q, do, doc, gain, w, fl, fm, fmo):
    sds = jax.ShapeDtypeStruct
    hbm = pl.BlockSpec(memory_space=pltpu.HBM)
    anywhere = pl.BlockSpec(memory_space=pl.ANY)
    vmem = pl.BlockSpec(memory_space=pltpu.VMEM)

    def v(shape, t):
        return pltpu.VMEM(shape, t)

    dma = pltpu.SemaphoreType.DMA
    scratch = [
        v((2 * TOK, HALF), bf16),
        v((TOK, HALF), bf16),
        v((HALF, 2 * TOK), bf16),
        v((TOK, WIDE), bf16),
        v((TOK, WIDE), bf16),
        v((TOK, 1024), bf16),
        v((GROUPS, HALF, 256), bf16),
        v((GROUPS, TOK, 256), bf16),
        v((GROUPS, TOK, 256), bf16),
        v((GROUPS, TOK, 256), f32),
        v((GROUPS, 2 * TOK, 256), bf16),
        v((PIECES, TOK, PIECE), bf16),
        v((PIECES, TOK, PIECE), bf16),
        v((32, TOK, 256), bf16),
        v((32, TOK, 256), bf16),
        v((TOK, HD), f32),
        v((TOK, HD), f32),
        v((TOK, HD), f32),
        v((TOK, HD), f32),
        v((128, 256), f32),
        v((256, 256), f32),
        v((TOK, HD), bf16),
        v((TOK, HD), bf16),
        v((HD, TOK), bf16),
        v((TOK, HD), f32),
        v((TOK, HD), f32),
        v((TOK, HD), f32),
        v((TOK, HD), f32),
        v((256, 1024), bf16),
        v((128, 1024), bf16),
        v((128, 1024), bf16),
        v((3, 128, 256), bf16),
        v((128, 128), bf16),
        v((128, 128), bf16),
        v((256, 1024), bf16),
        v((128, 256), f32),
        v((256, 128), f32),
        v((128, 128), f32),
        v((128, 128), f32),
        v((128, 128), f32),
        v((256, 128), f32),
        v((1, 256), jnp.int32),
        v((1, 256), bf16),
        dma((32,)), dma((32,)), dma((32,)), dma((32,)),
        dma((4,)), dma((4,)), dma((4,)), dma((4,)),
        dma((4,)), dma((4,)), dma((4,)), dma((4,)),
        dma((12,)), dma((12,)), dma((10,)),
    ]
    shapes = (
        sds((TOK, WIDE), bf16),
        sds((TOK, WIDE), bf16),
        sds((1, 256, 1024), f32),
        sds((1, 256), f32),
        sds((64, 256), f32),
        sds((64, 256), f32),
        sds((1, 256, 1024), bf16),
    )
    results = pl.pallas_call(
        kernel,
        out_shape=tuple(pltpu.VMEM(a.shape, a.dtype) for a in shapes),
        in_specs=[hbm] * 9,
        out_specs=(vmem,) * 7,
        scratch_shapes=scratch,
        compiler_params=pltpu.CompilerParams(
            collective_id=0, has_side_effects=True, vmem_limit_bytes=VMEM_LIMIT
        ),
        name="step",
    )(*(pltpu.with_memory_space_constraint(a, pltpu.HBM) for a in (x, q, do, doc, gain, w, fl, fm.T, fmo.T)))
    dq, dx, dw, dg, mn, mo, fn = pl.pallas_call(
        store,
        out_shape=shapes,
        in_specs=[anywhere] * 7,
        out_specs=(hbm,) * 7,
        scratch_shapes=[dma((7,))],
        compiler_params=pltpu.CompilerParams(vmem_limit_bytes=2**20),
        name="store",
    )(*results)
    return dq, dx, dw, dg, mn.T, mo.T, fn


def solution(mesh):
    placed = (
        P(("rep", "fsdp"), None),
        P(("rep", "fsdp"), None),
        P(("rep", "fsdp"), None),
        P(("rep", "fsdp"), None),
        P("rep", "fsdp"),
        P("rep", "fsdp", None),
        P("rep", "fsdp", None),
        P("fsdp", "rep"),
        P("fsdp", "rep"),
    )
    return jax.shard_map(
        on_device,
        mesh=mesh,
        in_specs=placed,
        out_specs=(
            P(("rep", "fsdp"), None),
            P(("rep", "fsdp"), None),
            P("rep", "fsdp", None),
            P("rep", "fsdp"),
            P("fsdp", "rep"),
            P("fsdp", "rep"),
            P("rep", "fsdp", None),
        ),
        check_vma=False,
    )
```

```python
import math

import jax
import jax.numpy as jnp
from jax import lax
from jax.experimental import pallas as pl
from jax.experimental.pallas import tpu as pltpu
from jax.sharding import PartitionSpec as P

epsilon = 1e-05
rope_base = 500000.0
outer_rate = 0.7
outer_momentum = 0.9
mixing = 0.5
masked_score = -1e30

TOK = 256
WIDE = 4096
HALF = 2048
GROUPS = 4
QUAD = 512
HD = 128
RING = 8
SCALE = HD ** (-0.5)
EXP2_SCALE = SCALE * math.log2(math.e)
PIECE = 512
PIECES = HALF // PIECE

f32 = jnp.float32
bf16 = jnp.bfloat16
VMEM_LIMIT = 44 * 2**20
NT = (((1,), (1,)), ((), ()))


BEFORE = (
    ("inv",), ("tab",), ("tr", 0, 0), ("tr", 0, 1), ("tr", 0, 2), ("tr", 0, 3), ("o", 1),
    ("ag", 0, 0, 0, 1), ("ag", 1, 0, 1, 1), ("ag", 0, 0, 1, 1), ("ag", 1, 0, 0, 1), ("o", 2),
    ("ag", 0, 1, 0, 1), ("ag", 1, 1, 1, 1), ("tr", 1, 0), ("ag", 0, 1, 1, 1), ("ag", 1, 1, 0, 1),
    ("ag", 0, 0, 0, 2), ("ag", 1, 0, 1, 2), ("ag", 0, 0, 1, 2), ("ag", 1, 0, 0, 2), ("o", 3),
    ("ag", 0, 1, 0, 2), ("ag", 1, 1, 1, 2), ("own", 2), ("tr", 1, 1), ("ag", 0, 1, 1, 2),
    ("ag", 1, 1, 0, 2), ("ag", 0, 0, 0, 3), ("ag", 1, 0, 1, 3), ("ag", 0, 0, 1, 3), ("ag", 1, 0, 0, 3),
    ("ag", 0, 1, 0, 3), ("ag", 1, 1, 1, 3), ("own", 3), ("tr", 1, 2), ("ag", 0, 2, 0, 1),
    ("ag", 1, 2, 1, 1), ("ag", 0, 2, 1, 1), ("ag", 1, 2, 0, 1), ("ag", 0, 1, 1, 3), ("ag", 1, 1, 0, 3),
    ("ag", 0, 0, 0, 4), ("ag", 1, 0, 1, 4), ("po", 0), ("pp", 0), ("ag", 0, 1, 0, 4),
    ("ag", 1, 1, 1, 4), ("pp", 1), ("po", 1), ("tr", 1, 3), ("o", 4), ("ag", 0, 3, 0, 1),
    ("ag", 1, 3, 1, 1), ("ag", 0, 3, 1, 1), ("ag", 1, 3, 0, 1), ("ag", 0, 2, 0, 2), ("ag", 1, 2, 1, 2),
    ("gs", 0),
)
DURING = (
    (),
    (
        ("ag", 0, 2, 1, 2), ("ag", 1, 2, 0, 2),
    ),
    (
        ("ag", 0, 3, 0, 2), ("ag", 1, 3, 1, 2), ("ge", 0), ("dq", 0), ("gs", 1), ("ag", 0, 3, 1, 2),
        ("ag", 1, 3, 0, 2),
    ),
    (),
    (
        ("ag", 0, 2, 0, 3), ("ag", 1, 2, 1, 3), ("ge", 1), ("dq", 1), ("ag", 0, 2, 1, 3),
        ("ag", 1, 2, 0, 3), ("dq", 2), ("dq", 3), ("o", 5), ("ag", 0, 3, 0, 3), ("ag", 1, 3, 1, 3),
        ("ew", 0), ("rs", 0, 0, 1, 1), ("rs", 1, 0, 0, 1), ("rs", 0, 0, 0, 1), ("rs", 1, 0, 1, 1),
        ("ag", 0, 3, 1, 3), ("ag", 1, 3, 0, 3), ("ag", 0, 2, 0, 4), ("ag", 1, 2, 1, 4), ("pp", 2),
        ("po", 2), ("ew", 1), ("rs", 0, 1, 1, 1), ("rs", 1, 1, 0, 1), ("rs", 0, 1, 0, 1),
        ("rs", 1, 1, 1, 1), ("ag", 0, 3, 0, 4), ("ag", 1, 3, 1, 4), ("pp", 3), ("po", 3),
        ("rs", 0, 0, 1, 2), ("rs", 1, 0, 0, 2), ("o", 6), ("rs", 0, 0, 0, 2), ("rs", 1, 0, 1, 2),
        ("gs", 2), ("rs", 0, 1, 1, 2), ("rs", 1, 1, 0, 2),
    ),
    (),
    (
        ("rs", 0, 1, 0, 2), ("rs", 1, 1, 1, 2), ("ge", 2), ("gs", 3), ("rs", 0, 0, 1, 3),
        ("rs", 1, 0, 0, 3),
    ),
    (),
)
AFTER = (
    ("rs", 0, 0, 0, 3), ("rs", 1, 0, 1, 3), ("ge", 3), ("rs", 0, 1, 1, 3), ("rs", 1, 1, 0, 3),
    ("uo", 0), ("uo", 1), ("uo", 2), ("rs", 0, 1, 0, 3), ("rs", 1, 1, 1, 3), ("uo", 3), ("ew", 2),
    ("rs", 0, 2, 1, 1), ("rs", 1, 2, 0, 1), ("rs", 0, 2, 0, 1), ("rs", 1, 2, 1, 1), ("dq", 4),
    ("dq", 5), ("dq", 6), ("rs", 0, 0, 0, 4), ("rs", 1, 0, 1, 4), ("dq", 7), ("ew", 3), ("us", 0),
    ("rs", 0, 3, 1, 1), ("rs", 1, 3, 0, 1), ("rs", 0, 3, 0, 1), ("rs", 1, 3, 1, 1), ("us", 1),
    ("us", 2), ("us", 3), ("rs", 0, 1, 0, 4), ("rs", 1, 1, 1, 4), ("o", 7), ("rs", 0, 2, 1, 2),
    ("rs", 1, 2, 0, 2), ("rs", 0, 2, 0, 2), ("rs", 1, 2, 1, 2), ("re", 0), ("rs", 0, 3, 1, 2),
    ("rs", 1, 3, 0, 2), ("ui", 0), ("rs", 0, 3, 0, 2), ("rs", 1, 3, 1, 2), ("re", 1),
    ("rs", 0, 2, 1, 3), ("rs", 1, 2, 0, 3), ("rs", 0, 2, 0, 3), ("rs", 1, 2, 1, 3), ("ui", 1),
    ("rs", 0, 3, 1, 3), ("rs", 1, 3, 0, 3), ("rs", 0, 3, 0, 3), ("rs", 1, 3, 1, 3), ("rs", 0, 2, 0, 4),
    ("rs", 1, 2, 1, 4), ("ui", 2), ("rs", 0, 3, 0, 4), ("rs", 1, 3, 1, 4), ("re", 2), ("ui", 3),
    ("re", 3),
)


def dot(a, b):
    return jnp.dot(a, b, preferred_element_type=f32)


def dot_nt(a, b):
    return lax.dot_general(a, b, NT, preferred_element_type=f32)


def kernel(
    x_ref, q_ref, do_ref, doc_ref, gain_ref, w_ref, fl_ref, fm_ref, fmo_ref,
    dq_out, dx_out, dw_out, dg_out, mn_out, mo_out, fn_out,
    X, XO, XT, Q, DO, WR, WB, PIN, POUT, PRAW, E, UOUT, UIN, RB, SB,
    INV, CO, COS, SIN, BLO, BHI, DSH, DSL, KB, VB, KT, DKA, DVA, GC, GT,
    F, FS, FSUM, XR, YS, YR, MW, M01, MB, MSB, R1, R2, PK, DOC, GAIN,
    ag_s, ag_r, rs_s, rs_r, x_s, x_r, p_s, p_r, e_s, e_r, u_s, u_r, o_s, o_r, l_s,
):
    f = lax.axis_index("fsdp")
    r = lax.axis_index("rep")
    z = lax.rem(f, RING)
    h = lax.div(f, RING)
    core = lax.rem(r, 2)
    yh = lax.rem(lax.div(r, 2), 2)
    xx = lax.div(r, 4)

    right = {"fsdp": h * RING + lax.rem(z + 1, RING)}
    left = {"fsdp": h * RING + lax.rem(z + RING - 1, RING)}
    partner = {"fsdp": (1 - h) * RING + z}
    sibling = {"rep": xx * 4 + yh * 2 + (1 - core)}
    across = {"rep": xx * 4 + (1 - yh) * 2 + core}
    xpeer = [{"rep": lax.rem(xx + j, 4) * 4 + yh * 2 + core} for j in (1, 2, 3)]

    def remote(src, dst, ssem, rsem, device):
        return pltpu.make_async_remote_copy(
            src_ref=src, dst_ref=dst, send_sem=ssem, recv_sem=rsem,
            device_id=device, device_id_type=pl.DeviceIdType.MESH,
        )

    def al(value, m):
        return pl.multiple_of(value, m)

    mine = pl.ds(al(h * HALF, HALF), HALF)
    other = pl.ds(al((1 - h) * HALF, HALF), HALF)
    ld_w = pltpu.make_async_copy(w_ref.at[0], WR, l_s.at[0])
    ld_x = pltpu.make_async_copy(x_ref.at[:, mine], X.at[0:TOK], l_s.at[1])
    ld_xo = pltpu.make_async_copy(x_ref.at[:, other], XO, l_s.at[2])
    ld_q = pltpu.make_async_copy(q_ref, Q, l_s.at[3])
    ld_do = pltpu.make_async_copy(do_ref, DO, l_s.at[4])
    ld_f = pltpu.make_async_copy(fl_ref.at[0], F, l_s.at[5])
    ld_m0 = pltpu.make_async_copy(fm_ref, M01.at[0:64], l_s.at[6])
    ld_m1 = pltpu.make_async_copy(fmo_ref, M01.at[64:128], l_s.at[7])
    ld_doc = pltpu.make_async_copy(doc_ref, DOC, l_s.at[8])
    ld_gain = pltpu.make_async_copy(gain_ref, GAIN, l_s.at[9])
    for c in (ld_w, ld_gain, ld_x, ld_xo, ld_f, ld_m0, ld_m1, ld_doc, ld_q, ld_do):
        c.start()

    barrier = pltpu.get_barrier_semaphore()
    for d in (left, right, partner, sibling, across, *xpeer):
        pl.semaphore_signal(barrier, inc=1, device_id=d, device_id_type=pl.DeviceIdType.MESH)

    def x_copy(j):
        return remote(
            x_ref.at[:, pl.ds(al((1 - h) * HALF + j * PIECE, PIECE), PIECE)],
            X.at[TOK : 2 * TOK, j * PIECE : (j + 1) * PIECE],
            x_s.at[j], x_r.at[j], partner,
        )

    def ring_at(dist):
        return lax.rem(z + dist + 2 * RING, RING)

    def hops(d, c):
        return RING // 2 if c == d else RING // 2 - 1

    def ring_sem(d, g, c, s):
        return ((d * GROUPS + g) * 2 + c) * 4 + s - 1

    def ag_copy(d, g, c, s, shard):
        block = WB.at[g, pl.ds(al(shard * TOK + c * 128, 128), 128)]
        i = ring_sem(d, g, c, s)
        return remote(block, block, ag_s.at[i], ag_r.at[i], (right, left)[d])

    def ag_send(d, g, c, s):
        return ag_copy(d, g, c, s, ring_at((1 - s) if d == 0 else (s - 1)))

    def ag_recv(d, g, c, s):
        return ag_copy(d, g, c, s, ring_at(-s if d == 0 else s))

    def ag_step(d, g, c, s):
        ag_recv(d, g, c, s).wait_recv()
        if s < hops(d, c):
            ag_send(d, g, c, s + 1).start()

    def ag_own(g):
        for c in (0, 1):
            for d in (0, 1):
                ag_send(d, g, c ^ d, 1).start()

    eye = lax.broadcasted_iota(jnp.int32, (TOK, TOK), 0) == lax.broadcasted_iota(jnp.int32, (TOK, TOK), 1)

    def column(row):
        square = jnp.where(eye, jnp.broadcast_to(row, (TOK, TOK)), 0.0).astype(bf16)
        return dot(square, jnp.ones((TOK, HD), bf16))

    ld_gain.wait()
    gain_row = GAIN[...].astype(f32)
    gain = column(gain_row)
    GC[...] = gain
    ld_w.wait()
    own_rows = pl.ds(al(z * TOK, TOK), TOK)

    def scale_w(g):
        WB[g, own_rows, 0:HD] = (WR[:, g * HD : (g + 1) * HD].astype(f32) * gain).astype(bf16)
        WB[g, own_rows, HD : 2 * HD] = (
            WR[:, 512 + g * HD : 512 + (g + 1) * HD].astype(f32) * gain
        ).astype(bf16)

    scale_w(0)
    pl.semaphore_wait(barrier, 8)
    for j in range(PIECES):
        x_copy(j).start()
    ag_own(0)
    scale_w(1)
    ag_own(1)
    scale_w(2)
    scale_w(3)

    rows_k = pl.ds(al(core * 128, 128), 128)
    rows_o = pl.ds(al((1 - core) * 128, 128), 128)
    lane = lax.broadcasted_iota(jnp.int32, (128, 128), 1)
    low = lane < 64
    block_c = pl.ds(al((2 * xx + yh) * 128, 128), 128)
    block_x = pl.ds(al(xx * 256, 256), 256)

    def swap(v):
        return pltpu.roll(v, 64, 1)

    o_frag = remote(F.at[rows_o], FS, o_s.at[0], o_r.at[0], sibling)
    o_state = remote(MB.at[rows_o], MSB, o_s.at[1], o_r.at[1], sibling)

    def o_x(j):
        to = lax.rem(xx + j + 1, 4)
        return remote(
            FSUM.at[:, pl.ds(al(to * 256, 256), 256)], XR.at[j], o_s.at[2 + j], o_r.at[2 + j], xpeer[j]
        )

    o_y = remote(YS, YR, o_s.at[5], o_r.at[5], across)
    o_pack = remote(R1, R2, o_s.at[6], o_r.at[6], sibling)

    def mw(rows, cols, i, device):
        return remote(MW.at[rows, cols], MW.at[rows, cols], o_s.at[i], o_r.at[i], device)

    o_back_y = mw(rows_k, block_c, 7, across)
    block_c_across = pl.ds(al((2 * xx + 1 - yh) * 128, 128), 128)
    o_back_y_in = mw(rows_k, block_c_across, 7, across)

    def o_back_x(j):
        return mw(rows_k, block_x, 8 + j, xpeer[j])

    def o_back_x_in(j):
        frm = lax.rem(xx + 4 - (j + 1), 4)
        return mw(rows_k, pl.ds(al(frm * 256, 256), 256), 8 + j, xpeer[j])

    o_back_s = mw(rows_k, slice(None), 11, sibling)
    o_back_s_in = mw(rows_o, slice(None), 11, sibling)

    def outer_1():
        ld_f.wait()
        ld_m0.wait()
        ld_m1.wait()
        MB[...] = M01[...].T
        o_frag.start()
        o_state.start()

    def outer_2():
        o_frag.wait_recv()
        FSUM[...] = (F[rows_k, :].astype(f32) + FS[...].astype(f32)).astype(bf16)
        for j in range(3):
            o_x(j).start()

    def outer_3():
        for j in range(3):
            o_x(j).wait_recv()
        total = FSUM[:, block_x].astype(f32)
        for j in range(3):
            total = total + XR[j].astype(f32)
        first, second = total[:, 0:128], total[:, 128:256]
        YS[...] = jnp.where(yh == 0, second, first).astype(bf16)
        R1[...] = jnp.where(yh == 0, first, second)
        o_y.start()

    def outer_4():
        o_y.wait_recv()
        o_state.wait_recv()
        mean = (R1[...] + YR[...].astype(f32)) * (1.0 / 16.0)
        own, sib = MB[rows_k, :], MSB[...]
        a = jnp.where(core == 0, own, sib)
        b = jnp.where(core == 0, sib, own)
        master = jnp.where(low, a, swap(b))
        moment = jnp.where(low, swap(a), b)
        pseudo = master - mean
        moment_next = outer_momentum * moment + pseudo
        master_next = master - outer_rate * (pseudo + outer_momentum * moment_next)
        MW[rows_k, block_c] = master_next.astype(bf16)
        o_back_y.start()
        pack_0 = jnp.where(low, master_next, swap(moment_next))
        pack_1 = jnp.where(low, swap(master_next), moment_next)
        R1[...] = jnp.where(core == 0, pack_1, pack_0)
        o_pack.start()
        keep = jnp.where(core == 0, pack_0, pack_1)
        PK[rows_k, :] = keep

    def outer_5():
        o_back_y_in.wait_recv()
        for j in range(3):
            o_back_x(j).start()
        o_pack.wait_recv()
        PK[rows_o, :] = R2[...]
        both = PK[...].T
        mn_out[...] = both[0:64]
        mo_out[...] = both[64:128]

    def outer_6():
        for j in range(3):
            o_back_x_in(j).wait_recv()
        o_back_s.start()

    def outer_7():
        o_back_s_in.wait_recv()
        fn_out[0] = (mixing * F[...].astype(f32) + (1.0 - mixing) * MW[...].astype(f32)).astype(bf16)

    def tables():
        ld_doc.wait()
        doc_row = DOC[...].astype(f32)
        doc = column(doc_row)
        doc2 = jnp.concatenate([doc, doc], axis=1)
        row = jnp.broadcast_to(doc_row, (TOK, TOK))
        before = jnp.sum(jnp.where(row < doc2, 1.0, 0.0), axis=1, keepdims=True)
        token = lax.broadcasted_iota(jnp.int32, (TOK, HD), 0).astype(f32)
        position = token - before
        i = lax.broadcasted_iota(jnp.int32, (TOK, HD), 1)
        half = jnp.where(i < 64, i, i - 64).astype(f32)
        angle = position * jnp.exp(half * (-2.0 / HD * math.log(rope_base)))
        COS[...] = jnp.cos(angle)
        SIN[...] = jnp.where(i < 64, -1.0, 1.0) * jnp.sin(angle)
        u = lax.broadcasted_iota(jnp.int32, (TOK, TOK), 0)
        t = lax.broadcasted_iota(jnp.int32, (TOK, TOK), 1)
        bias = jnp.where((u <= t) & (row == doc2), 0.0, masked_score)
        BLO[...] = jnp.concatenate([bias[0:128, 0:128]] * 4, axis=1)
        BHI[...] = jnp.concatenate([bias[:, 128:256]] * 4, axis=1)

    def inverse():
        ld_x.wait()
        ld_xo.wait()
        a = X[0:TOK, :].astype(f32)
        total = jnp.sum(a * a, axis=1, keepdims=True)
        b = XO[...].astype(f32)
        total = total + jnp.sum(b * b, axis=1, keepdims=True)
        INV[...] = jnp.broadcast_to(lax.rsqrt(total * (1.0 / WIDE) + epsilon), (TOK, HD))
        CO[...] = jnp.zeros_like(CO)

    def transpose_x(who, j):
        XT[j * PIECE : (j + 1) * PIECE, who * TOK : (who + 1) * TOK] = X[
            who * TOK : (who + 1) * TOK, j * PIECE : (j + 1) * PIECE
        ].T

    def p_copy(g):
        return remote(POUT.at[g], PIN.at[g], p_s.at[g], p_r.at[g], partner)

    def project_partner(g):
        POUT[g] = dot(X[TOK : 2 * TOK, :], WB[g]).astype(bf16)
        p_copy(g).start()

    def project_own(g):
        PRAW[g] = dot(X[0:TOK, :], WB[g])

    def e_copy(g):
        return remote(E.at[g, 0:TOK], E.at[g, TOK : 2 * TOK], e_s.at[g], e_r.at[g], partner)

    def group_start(g):
        p_copy(g).wait_recv()
        raw = PRAW[g] + PIN[g].astype(f32)
        PRAW[g] = raw
        inv = INV[...]
        k = raw[:, 0:HD] * inv
        k = k * COS[...] + pltpu.roll(k, 64, 1) * SIN[...]
        kb = k.astype(bf16)
        KB[...] = kb
        KT[g] = kb.T
        VB[...] = (raw[:, HD : 2 * HD] * inv).astype(bf16)
        DKA[...] = jnp.zeros_like(DKA)
        DVA[...] = jnp.zeros_like(DVA)

    def group_end(g):
        dk = DKA[...] * SCALE
        inv = INV[...]
        dk = dk * COS[...] - pltpu.roll(dk, 64, 1) * SIN[...]
        ek = (dk * inv).astype(bf16)
        ev = (DVA[...] * inv).astype(bf16)
        E[g, 0:TOK, 0:HD] = ek
        E[g, 0:TOK, HD : 2 * HD] = ev
        e_copy(g).start()
        raw = PRAW[g]
        part = ek.astype(f32) * raw[:, 0:HD] + ev.astype(f32) * raw[:, HD : 2 * HD]
        CO[...] += jnp.broadcast_to(jnp.sum(part, axis=1, keepdims=True), (TOK, HD))

    low_rows, high_rows = slice(0, 128), slice(128, 256)

    def softmax(s, w):
        top = jnp.max(s, axis=0, keepdims=True)
        e = jnp.exp2((s - top) * EXP2_SCALE)
        p = e * (1.0 / jnp.sum(e, axis=0, keepdims=True))
        pw = p * w
        delta = jnp.sum(pw, axis=0, keepdims=True)
        return p.astype(bf16), (pw - p * delta).astype(bf16)

    def heads(n):
        def rows_of(ref, rows):
            return jnp.concatenate(
                [ref[rows, pl.ds(al(n * QUAD + i * HD, HD), HD)] for i in range(4)], axis=0
            )

        q_high, d_high = rows_of(Q, high_rows), rows_of(DO, high_rows)
        q_low, d_low = rows_of(Q, low_rows), rows_of(DO, low_rows)
        kb, vb = KB[...], VB[...]
        s_high, w_high = dot_nt(kb, q_high) + BHI[...], dot_nt(vb, d_high)
        s_low, w_low = dot_nt(kb[low_rows], q_low) + BLO[...], dot_nt(vb[low_rows], d_low)
        p_high, ds_high = softmax(s_high, w_high)
        p_low, ds_low = softmax(s_low, w_low)
        DSH[n] = ds_high
        DSL[n] = ds_low
        DKA[...] += dot(ds_high, q_high)
        DVA[...] += dot(p_high, d_high)
        DKA[low_rows, :] += dot(ds_low, q_low)
        DVA[low_rows, :] += dot(p_low, d_low)

    def query_gradient(n):
        g = n // 2
        for rows, ds in ((high_rows, DSH[n]), (low_rows, DSL[n])):
            kt = KT[g] if rows is high_rows else KT[g, :, 0:128]
            dq = (dot(kt, ds) * SCALE).T.astype(bf16)
            for i in range(4):
                c = n * QUAD + i * HD
                dq_out[rows, c : c + HD] = dq[i * 128 : (i + 1) * 128]

    def rs_copy(d, g, c, s):
        i = ring_sem(d, g, c, s)
        return remote(SB.at[i], RB.at[i], rs_s.at[i], rs_r.at[i], (right, left)[d])

    def rs_step(d, g, c, s):
        far = hops(d, c) + 1 - s
        owner = ring_at(far if d == 0 else -far)
        i = ring_sem(d, g, c, s)
        total = dot(XT[pl.ds(al(owner * TOK + c * 128, 128), 128), :], E[g])
        if s > 1:
            rs_copy(d, g, c, s - 1).wait_recv()
            total = total + RB[i - 1].astype(f32)
        SB[i] = total.astype(bf16)
        rs_copy(d, g, c, s).start()

    def rs_end(g):
        total = dot(XT[pl.ds(al(z * TOK, TOK), TOK), :], E[g])
        came = []
        for c in (0, 1):
            for d in (0, 1):
                rs_copy(d, g, c, hops(d, c)).wait_recv()
            first, second = (RB[ring_sem(d, g, c, hops(d, c))].astype(f32) for d in (0, 1))
            came.append(first + second)
        total = total + jnp.concatenate(came, axis=0)
        ck, cv = g * HD, 512 + g * HD
        wide_gain = GC[...]
        tk, tv = total[:, 0:HD], total[:, HD : 2 * HD]
        dw_out[0, :, ck : ck + HD] = tk * wide_gain
        dw_out[0, :, cv : cv + HD] = tv * wide_gain
        part = tk * WR[:, ck : ck + HD].astype(f32) + tv * WR[:, cv : cv + HD].astype(f32)
        GT[...] += jnp.broadcast_to(jnp.sum(part, axis=1, keepdims=True), (TOK, HD))

    def u_copy(j):
        return remote(UOUT.at[j], UIN.at[j], u_s.at[j], u_r.at[j], partner)

    def upstream(first, j):
        rows = slice(j * PIECE, (j + 1) * PIECE)
        total = dot_nt(E[0, first : first + TOK], WB[0, rows])
        for g in range(1, GROUPS):
            total = total + dot_nt(E[g, first : first + TOK], WB[g, rows])
        return total

    def send_upstream(j):
        UOUT[j] = upstream(TOK, j).astype(bf16)
        u_copy(j).start()

    def finish(part, j, u):
        cols = slice(j * PIECE, (j + 1) * PIECE)
        x = X[0:TOK, cols] if part == 0 else XO[:, cols]
        c = CO[...]
        c = jnp.concatenate([c] * (PIECE // HD), axis=1)
        start = al((h if part == 0 else 1 - h) * HALF + j * PIECE, PIECE)
        dx_out[:, pl.ds(start, PIECE)] = (u - x.astype(f32) * c).astype(bf16)

    def outer(k):
        (outer_1, outer_2, outer_3, outer_4, outer_5, outer_6, outer_7)[k - 1]()

    def x_transpose(who, j):
        if who == 1 and j < PIECES - 1:
            x_copy(j).wait_recv()
        transpose_x(who, j)

    def start_group(g):
        if g == 0:
            ld_q.wait()
            ld_do.wait()
        group_start(g)

    def end_group(g):
        group_end(g)
        if g == GROUPS - 1:
            CO[...] = CO[...] * INV[...] * INV[...] * (1.0 / WIDE)

    def first_projection(g):
        if g == 0:
            x_copy(PIECES - 1).wait_recv()
        project_partner(g)

    def upstream_in(j):
        u_copy(j).wait_recv()
        finish(1, j, UIN[j].astype(f32))

    acts = dict(
        ag=ag_step, own=ag_own, tab=tables, inv=inverse, tr=x_transpose, pp=first_projection, po=project_own,
        gs=start_group, ge=end_group, rs=rs_step, ew=lambda g: e_copy(g).wait_recv(), re=rs_end, us=send_upstream,
        uo=lambda j: finish(0, j, upstream(0, j)), ui=upstream_in, o=outer, dq=query_gradient,
    )

    def play(items):
        for name, *numbers in items:
            acts[name](*numbers)

    GT[...] = jnp.zeros_like(GT)
    play(BEFORE)

    def step(n, _):
        for k, items in enumerate(DURING):
            if items:

                @pl.when(n == k)
                def _(items=items):
                    play(items)

        heads(n)
        return 0

    lax.fori_loop(0, GROUPS * 2, step, 0)
    play(AFTER)
    spread = jnp.where(eye, jnp.concatenate([GT[...], GT[...]], axis=1), 0.0)
    dg_out[...] = jnp.sum(spread, axis=0, keepdims=True)

    for j in range(PIECES):
        x_copy(j).wait_send()
        u_copy(j).wait_send()

    def drain(g, _):
        p_copy(g).wait_send()
        e_copy(g).wait_send()
        for d in (0, 1):
            for c in (0, 1):
                for s in range(1, hops(d, c) + 1):
                    ag_send(d, g, c, s).wait_send()
                    rs_copy(d, g, c, s).wait_send()
        return 0

    lax.fori_loop(0, GROUPS, drain, 0)
    for c in (o_frag, o_state, o_y, o_pack, o_back_y, o_back_s):
        c.wait_send()
    for j in range(3):
        o_x(j).wait_send()
        o_back_x(j).wait_send()


def store(*refs):
    n = len(refs) // 2
    sems = refs[-1]
    copies = [pltpu.make_async_copy(refs[i], refs[n + i], sems.at[i]) for i in range(n)]
    for c in copies:
        c.start()
    for c in copies:
        c.wait()


def on_device(x, q, do, doc, gain, w, fl, fm, fmo):
    sds = jax.ShapeDtypeStruct
    hbm = pl.BlockSpec(memory_space=pltpu.HBM)
    anywhere = pl.BlockSpec(memory_space=pl.ANY)
    vmem = pl.BlockSpec(memory_space=pltpu.VMEM)

    def v(shape, t):
        return pltpu.VMEM(shape, t)

    dma = pltpu.SemaphoreType.DMA
    scratch = [
        v((2 * TOK, HALF), bf16),
        v((TOK, HALF), bf16),
        v((HALF, 2 * TOK), bf16),
        v((TOK, WIDE), bf16),
        v((TOK, WIDE), bf16),
        v((TOK, 1024), bf16),
        v((GROUPS, HALF, 256), bf16),
        v((GROUPS, TOK, 256), bf16),
        v((GROUPS, TOK, 256), bf16),
        v((GROUPS, TOK, 256), f32),
        v((GROUPS, 2 * TOK, 256), bf16),
        v((PIECES, TOK, PIECE), bf16),
        v((PIECES, TOK, PIECE), bf16),
        v((64, 128, 256), bf16),
        v((64, 128, 256), bf16),
        v((TOK, HD), f32),
        v((TOK, HD), f32),
        v((TOK, HD), f32),
        v((TOK, HD), f32),
        v((128, 512), f32),
        v((256, 512), f32),
        v((8, 256, 512), bf16),
        v((8, 128, 512), bf16),
        v((TOK, HD), bf16),
        v((TOK, HD), bf16),
        v((GROUPS, HD, TOK), bf16),
        v((TOK, HD), f32),
        v((TOK, HD), f32),
        v((TOK, HD), f32),
        v((TOK, HD), f32),
        v((256, 1024), bf16),
        v((128, 1024), bf16),
        v((128, 1024), bf16),
        v((3, 128, 256), bf16),
        v((128, 128), bf16),
        v((128, 128), bf16),
        v((256, 1024), bf16),
        v((128, 256), f32),
        v((256, 128), f32),
        v((128, 128), f32),
        v((128, 128), f32),
        v((128, 128), f32),
        v((256, 128), f32),
        v((1, 256), jnp.int32),
        v((1, 256), bf16),
        dma((64,)), dma((64,)), dma((64,)), dma((64,)),
        dma((4,)), dma((4,)), dma((4,)), dma((4,)),
        dma((4,)), dma((4,)), dma((4,)), dma((4,)),
        dma((12,)), dma((12,)), dma((10,)),
    ]
    shapes = (
        sds((TOK, WIDE), bf16),
        sds((TOK, WIDE), bf16),
        sds((1, 256, 1024), f32),
        sds((1, 256), f32),
        sds((64, 256), f32),
        sds((64, 256), f32),
        sds((1, 256, 1024), bf16),
    )
    results = pl.pallas_call(
        kernel,
        out_shape=tuple(pltpu.VMEM(a.shape, a.dtype) for a in shapes),
        in_specs=[hbm] * 9,
        out_specs=(vmem,) * 7,
        scratch_shapes=scratch,
        compiler_params=pltpu.CompilerParams(
            collective_id=0, has_side_effects=True, vmem_limit_bytes=VMEM_LIMIT
        ),
        name="step",
    )(*(pltpu.with_memory_space_constraint(a, pltpu.HBM) for a in (x, q, do, doc, gain, w, fl, fm.T, fmo.T)))
    dq, dx, dw, dg, mn, mo, fn = pl.pallas_call(
        store,
        out_shape=shapes,
        in_specs=[anywhere] * 7,
        out_specs=(hbm,) * 7,
        scratch_shapes=[dma((7,))],
        compiler_params=pltpu.CompilerParams(vmem_limit_bytes=2**20),
        name="store",
    )(*results)
    return dq, dx, dw, dg, mn.T, mo.T, fn


def solution(mesh):
    placed = (
        P(("rep", "fsdp"), None),
        P(("rep", "fsdp"), None),
        P(("rep", "fsdp"), None),
        P(("rep", "fsdp"), None),
        P("rep", "fsdp"),
        P("rep", "fsdp", None),
        P("rep", "fsdp", None),
        P("fsdp", "rep"),
        P("fsdp", "rep"),
    )
    return jax.shard_map(
        on_device,
        mesh=mesh,
        in_specs=placed,
        out_specs=(
            P(("rep", "fsdp"), None),
            P(("rep", "fsdp"), None),
            P("rep", "fsdp", None),
            P("rep", "fsdp"),
            P("fsdp", "rep"),
            P("fsdp", "rep"),
            P("rep", "fsdp", None),
        ),
        check_vma=False,
    )
```

```python
import math

import jax
import jax.numpy as jnp
from jax import lax
from jax.experimental import pallas as pl
from jax.experimental.pallas import tpu as pltpu
from jax.sharding import PartitionSpec as P

epsilon = 1e-05
rope_base = 500000.0
outer_rate = 0.7
outer_momentum = 0.9
mixing = 0.5
masked_score = -1e30

TOK = 256
WIDE = 4096
HALF = 2048
GROUPS = 4
QUAD = 512
HD = 128
RING = 8
SCALE = HD ** (-0.5)
EXP2_SCALE = SCALE * math.log2(math.e)
PIECE = 512
PIECES = HALF // PIECE

f32 = jnp.float32
bf16 = jnp.bfloat16
STORE_PARTS = 4
VMEM_LIMIT = 44 * 2**20
NT = (((1,), (1,)), ((), ()))


BEFORE = (
    ("inv",), ("tab",), ("tr", 0, 0), ("tr", 0, 1), ("tr", 0, 2), ("tr", 0, 3), ("o", 1),
    ("ag", 0, 0, 0, 1), ("ag", 1, 0, 1, 1), ("ag", 0, 0, 1, 1), ("ag", 1, 0, 0, 1), ("o", 2),
    ("ag", 0, 1, 0, 1), ("ag", 1, 1, 1, 1), ("ag", 0, 1, 1, 1), ("ag", 1, 1, 0, 1), ("tr", 1, 0),
    ("ag", 0, 0, 0, 2), ("ag", 1, 0, 1, 2), ("ag", 0, 0, 1, 2), ("ag", 1, 0, 0, 2), ("ag", 0, 1, 0, 2),
    ("ag", 1, 1, 1, 2), ("own", 2), ("o", 3), ("ag", 0, 1, 1, 2), ("ag", 1, 1, 0, 2), ("tr", 1, 1),
    ("ag", 0, 0, 0, 3), ("ag", 1, 0, 1, 3), ("ag", 0, 0, 1, 3), ("ag", 1, 0, 0, 3), ("ag", 0, 1, 0, 3),
    ("ag", 1, 1, 1, 3), ("own", 3), ("ag", 0, 2, 0, 1), ("ag", 1, 2, 1, 1), ("tr", 1, 2),
    ("ag", 0, 2, 1, 1), ("ag", 1, 2, 0, 1), ("ag", 0, 1, 1, 3), ("ag", 1, 1, 0, 3), ("ag", 0, 0, 0, 4),
    ("ag", 1, 0, 1, 4), ("po", 0), ("ag", 0, 1, 0, 4), ("ag", 1, 1, 1, 4), ("po", 1), ("pp", 0),
    ("pp", 1), ("tr", 1, 3), ("ag", 0, 3, 0, 1), ("ag", 1, 3, 1, 1), ("o", 4), ("ag", 0, 3, 1, 1),
    ("ag", 1, 3, 0, 1), ("ag", 0, 2, 0, 2), ("ag", 1, 2, 1, 2), ("ag", 0, 2, 1, 2), ("ag", 1, 2, 0, 2),
    ("gs", 0),
)
DURING = (
    (),
    (),
    (
        ("ag", 0, 3, 0, 2), ("ag", 1, 3, 1, 2), ("ge", 0), ("dq", 0), ("ag", 0, 3, 1, 2),
        ("ag", 1, 3, 0, 2), ("gs", 1),
    ),
    (
        ("ag", 0, 2, 0, 3), ("ag", 1, 2, 1, 3),
    ),
    (
        ("ag", 0, 2, 1, 3), ("ag", 1, 2, 0, 3), ("ge", 1), ("dq", 1), ("dq", 2), ("ag", 0, 3, 0, 3),
        ("ag", 1, 3, 1, 3), ("dq", 3), ("ew", 0), ("rs", 0, 0, 1, 1), ("rs", 1, 0, 0, 1),
        ("rs", 0, 0, 0, 1), ("rs", 1, 0, 1, 1), ("o", 5), ("ag", 0, 3, 1, 3), ("ag", 1, 3, 0, 3),
        ("ag", 0, 2, 0, 4), ("ag", 1, 2, 1, 4), ("pp", 2), ("po", 2), ("ew", 1), ("rs", 0, 1, 1, 1),
        ("rs", 1, 1, 0, 1), ("ag", 0, 3, 0, 4), ("ag", 1, 3, 1, 4), ("rs", 0, 1, 0, 1), ("rs", 1, 1, 1, 1),
        ("pp", 3), ("po", 3), ("rs", 0, 0, 1, 2), ("rs", 1, 0, 0, 2), ("rs", 0, 0, 0, 2),
        ("rs", 1, 0, 1, 2), ("o", 6), ("gs", 2), ("rs", 0, 1, 1, 2), ("rs", 1, 1, 0, 2),
    ),
    (),
    (
        ("rs", 0, 1, 0, 2), ("rs", 1, 1, 1, 2), ("ge", 2), ("gs", 3), ("rs", 0, 0, 1, 3),
        ("rs", 1, 0, 0, 3),
    ),
    (),
)
AFTER = (
    ("rs", 0, 0, 0, 3), ("rs", 1, 0, 1, 3), ("ge", 3), ("rs", 0, 1, 1, 3), ("rs", 1, 1, 0, 3),
    ("uo", 0), ("uo", 1), ("uo", 2), ("rs", 0, 1, 0, 3), ("rs", 1, 1, 1, 3), ("uo", 3), ("ew", 2),
    ("rs", 0, 2, 1, 1), ("rs", 1, 2, 0, 1), ("rs", 0, 2, 0, 1), ("rs", 1, 2, 1, 1), ("dq", 4),
    ("dq", 5), ("dq", 6), ("rs", 0, 0, 0, 4), ("rs", 1, 0, 1, 4), ("dq", 7), ("ew", 3), ("us", 0),
    ("rs", 0, 3, 1, 1), ("rs", 1, 3, 0, 1), ("rs", 0, 3, 0, 1), ("rs", 1, 3, 1, 1), ("us", 1),
    ("us", 2), ("us", 3), ("rs", 0, 1, 0, 4), ("rs", 1, 1, 1, 4), ("o", 7), ("rs", 0, 2, 1, 2),
    ("rs", 1, 2, 0, 2), ("rs", 0, 2, 0, 2), ("rs", 1, 2, 1, 2), ("re", 0), ("rs", 0, 3, 1, 2),
    ("rs", 1, 3, 0, 2), ("ui", 0), ("dr", 0), ("rs", 0, 3, 0, 2), ("rs", 1, 3, 1, 2), ("re", 1),
    ("rs", 0, 2, 1, 3), ("rs", 1, 2, 0, 3), ("rs", 0, 2, 0, 3), ("rs", 1, 2, 1, 3), ("ui", 1), ("dr", 1),
    ("rs", 0, 3, 1, 3), ("rs", 1, 3, 0, 3), ("rs", 0, 3, 0, 3), ("rs", 1, 3, 1, 3), ("rs", 0, 2, 0, 4),
    ("rs", 1, 2, 1, 4), ("ui", 2), ("rs", 0, 3, 0, 4), ("rs", 1, 3, 1, 4), ("re", 2), ("ui", 3),
    ("dr", 2), ("re", 3),
)


def dot(a, b):
    return jnp.dot(a, b, preferred_element_type=f32)


def dot_nt(a, b):
    return lax.dot_general(a, b, NT, preferred_element_type=f32)


def kernel(
    x_ref, q_ref, do_ref, doc_ref, gain_ref, w_ref, fl_ref, fm_ref, fmo_ref,
    dq_out, dx_out, dw_out, dg_out, mn_out, mo_out, fn_out,
    X, XO, XT, Q, DO, WR, WB, PIN, POUT, PRAW, E, UOUT, UIN, RB, SB,
    INV, CO, COS, SIN, BLO, BHI, DSH, DSL, KB, VB, KT, DKA, DVA, GC, GT,
    F, FS, FSUM, XR, YS, YR, MW, M01, MB, MSB, R1, R2, PK, DOC, GAIN,
    ag_s, ag_r, rs_s, rs_r, x_s, x_r, p_s, p_r, e_s, e_r, u_s, u_r, o_s, o_r, l_s,
):
    f = lax.axis_index("fsdp")
    r = lax.axis_index("rep")
    z = lax.rem(f, RING)
    h = lax.div(f, RING)
    core = lax.rem(r, 2)
    yh = lax.rem(lax.div(r, 2), 2)
    xx = lax.div(r, 4)

    right = {"fsdp": h * RING + lax.rem(z + 1, RING)}
    left = {"fsdp": h * RING + lax.rem(z + RING - 1, RING)}
    partner = {"fsdp": (1 - h) * RING + z}
    sibling = {"rep": xx * 4 + yh * 2 + (1 - core)}
    across = {"rep": xx * 4 + (1 - yh) * 2 + core}
    xpeer = [{"rep": lax.rem(xx + j, 4) * 4 + yh * 2 + core} for j in (1, 2, 3)]

    def remote(src, dst, ssem, rsem, device):
        return pltpu.make_async_remote_copy(
            src_ref=src, dst_ref=dst, send_sem=ssem, recv_sem=rsem,
            device_id=device, device_id_type=pl.DeviceIdType.MESH,
        )

    def al(value, m):
        return pl.multiple_of(value, m)

    mine = pl.ds(al(h * HALF, HALF), HALF)
    other = pl.ds(al((1 - h) * HALF, HALF), HALF)
    ld_w = pltpu.make_async_copy(w_ref.at[0], WR, l_s.at[0])
    ld_x = pltpu.make_async_copy(x_ref.at[:, mine], X.at[0:TOK], l_s.at[1])
    ld_xo = pltpu.make_async_copy(x_ref.at[:, other], XO, l_s.at[2])
    ld_q = pltpu.make_async_copy(q_ref, Q, l_s.at[3])
    ld_do = pltpu.make_async_copy(do_ref, DO, l_s.at[4])
    ld_f = pltpu.make_async_copy(fl_ref.at[0], F, l_s.at[5])
    ld_m0 = pltpu.make_async_copy(fm_ref, M01.at[0:64], l_s.at[6])
    ld_m1 = pltpu.make_async_copy(fmo_ref, M01.at[64:128], l_s.at[7])
    ld_doc = pltpu.make_async_copy(doc_ref, DOC, l_s.at[8])
    ld_gain = pltpu.make_async_copy(gain_ref, GAIN, l_s.at[9])
    ld_gain.start()
    ld_w.start()
    barrier = pltpu.get_barrier_semaphore()
    for d in (left, right, partner, sibling, across, *xpeer):
        pl.semaphore_signal(barrier, inc=1, device_id=d, device_id_type=pl.DeviceIdType.MESH)

    def x_copy(j):
        return remote(
            x_ref.at[:, pl.ds(al((1 - h) * HALF + j * PIECE, PIECE), PIECE)],
            X.at[TOK : 2 * TOK, j * PIECE : (j + 1) * PIECE],
            x_s.at[j], x_r.at[j], partner,
        )

    def ring_at(dist):
        return lax.rem(z + dist + 2 * RING, RING)

    def hops(d, c):
        return RING // 2 if c == d else RING // 2 - 1

    def ring_sem(d, g, c, s):
        return ((d * GROUPS + g) * 2 + c) * 4 + s - 1

    def ag_copy(d, g, c, s, shard):
        block = WB.at[g, pl.ds(al(shard * TOK + c * 128, 128), 128)]
        i = ring_sem(d, g, c, s)
        return remote(block, block, ag_s.at[i], ag_r.at[i], (right, left)[d])

    def ag_send(d, g, c, s):
        return ag_copy(d, g, c, s, ring_at((1 - s) if d == 0 else (s - 1)))

    def ag_recv(d, g, c, s):
        return ag_copy(d, g, c, s, ring_at(-s if d == 0 else s))

    def ag_step(d, g, c, s):
        ag_recv(d, g, c, s).wait_recv()
        if s < hops(d, c):
            ag_send(d, g, c, s + 1).start()

    def ag_own(g):
        for c in (0, 1):
            for d in (0, 1):
                ag_send(d, g, c ^ d, 1).start()

    eye = lax.broadcasted_iota(jnp.int32, (TOK, TOK), 0) == lax.broadcasted_iota(jnp.int32, (TOK, TOK), 1)

    def column(row):
        square = jnp.where(eye, jnp.broadcast_to(row, (TOK, TOK)), 0.0).astype(bf16)
        return dot(square, jnp.ones((TOK, HD), bf16))

    ld_gain.wait()
    gain_row = GAIN[...].astype(f32)
    gain = column(gain_row)
    GC[...] = gain
    ld_w.wait()
    own_rows = pl.ds(al(z * TOK, TOK), TOK)

    def scale_w(g):
        WB[g, own_rows, 0:HD] = (WR[:, g * HD : (g + 1) * HD].astype(f32) * gain).astype(bf16)
        WB[g, own_rows, HD : 2 * HD] = (
            WR[:, 512 + g * HD : 512 + (g + 1) * HD].astype(f32) * gain
        ).astype(bf16)

    scale_w(0)
    pl.semaphore_wait(barrier, 8)
    ag_own(0)
    for j in range(PIECES):
        x_copy(j).start()
    scale_w(1)
    ag_own(1)
    for c in (ld_x, ld_xo, ld_f, ld_m0, ld_m1, ld_doc, ld_q, ld_do):
        c.start()
    scale_w(2)
    scale_w(3)

    rows_k = pl.ds(al(core * 128, 128), 128)
    rows_o = pl.ds(al((1 - core) * 128, 128), 128)
    lane = lax.broadcasted_iota(jnp.int32, (128, 128), 1)
    low = lane < 64
    block_c = pl.ds(al((2 * xx + yh) * 128, 128), 128)
    block_x = pl.ds(al(xx * 256, 256), 256)

    def swap(v):
        return pltpu.roll(v, 64, 1)

    o_frag = remote(F.at[rows_o], FS, o_s.at[0], o_r.at[0], sibling)
    o_state = remote(MB.at[rows_o], MSB, o_s.at[1], o_r.at[1], sibling)

    def o_x(j):
        to = lax.rem(xx + j + 1, 4)
        return remote(
            FSUM.at[:, pl.ds(al(to * 256, 256), 256)], XR.at[j], o_s.at[2 + j], o_r.at[2 + j], xpeer[j]
        )

    o_y = remote(YS, YR, o_s.at[5], o_r.at[5], across)
    o_pack = remote(R1, R2, o_s.at[6], o_r.at[6], sibling)

    def mw(rows, cols, i, device):
        return remote(MW.at[rows, cols], MW.at[rows, cols], o_s.at[i], o_r.at[i], device)

    o_back_y = mw(rows_k, block_c, 7, across)
    block_c_across = pl.ds(al((2 * xx + 1 - yh) * 128, 128), 128)
    o_back_y_in = mw(rows_k, block_c_across, 7, across)

    def o_back_x(j):
        return mw(rows_k, block_x, 8 + j, xpeer[j])

    def o_back_x_in(j):
        frm = lax.rem(xx + 4 - (j + 1), 4)
        return mw(rows_k, pl.ds(al(frm * 256, 256), 256), 8 + j, xpeer[j])

    o_back_s = mw(rows_k, slice(None), 11, sibling)
    o_back_s_in = mw(rows_o, slice(None), 11, sibling)

    def outer_1():
        ld_f.wait()
        ld_m0.wait()
        ld_m1.wait()
        MB[...] = M01[...].T
        o_frag.start()
        o_state.start()

    def outer_2():
        o_frag.wait_recv()
        FSUM[...] = (F[rows_k, :].astype(f32) + FS[...].astype(f32)).astype(bf16)
        for j in range(3):
            o_x(j).start()

    def outer_3():
        for j in range(3):
            o_x(j).wait_recv()
        total = FSUM[:, block_x].astype(f32)
        for j in range(3):
            total = total + XR[j].astype(f32)
        first, second = total[:, 0:128], total[:, 128:256]
        YS[...] = jnp.where(yh == 0, second, first).astype(bf16)
        R1[...] = jnp.where(yh == 0, first, second)
        o_y.start()

    def outer_4():
        o_y.wait_recv()
        o_state.wait_recv()
        mean = (R1[...] + YR[...].astype(f32)) * (1.0 / 16.0)
        own, sib = MB[rows_k, :], MSB[...]
        a = jnp.where(core == 0, own, sib)
        b = jnp.where(core == 0, sib, own)
        master = jnp.where(low, a, swap(b))
        moment = jnp.where(low, swap(a), b)
        pseudo = master - mean
        moment_next = outer_momentum * moment + pseudo
        master_next = master - outer_rate * (pseudo + outer_momentum * moment_next)
        MW[rows_k, block_c] = master_next.astype(bf16)
        o_back_y.start()
        pack_0 = jnp.where(low, master_next, swap(moment_next))
        pack_1 = jnp.where(low, swap(master_next), moment_next)
        R1[...] = jnp.where(core == 0, pack_1, pack_0)
        o_pack.start()
        keep = jnp.where(core == 0, pack_0, pack_1)
        PK[rows_k, :] = keep

    def outer_5():
        o_back_y_in.wait_recv()
        for j in range(3):
            o_back_x(j).start()
        o_pack.wait_recv()
        PK[rows_o, :] = R2[...]
        both = PK[...].T
        mn_out[...] = both[0:64]
        mo_out[...] = both[64:128]

    def outer_6():
        for j in range(3):
            o_back_x_in(j).wait_recv()
        o_back_s.start()

    def outer_7():
        o_back_s_in.wait_recv()
        fn_out[0] = (mixing * F[...].astype(f32) + (1.0 - mixing) * MW[...].astype(f32)).astype(bf16)

    def tables():
        ld_doc.wait()
        doc_row = DOC[...].astype(f32)
        doc = column(doc_row)
        doc2 = jnp.concatenate([doc, doc], axis=1)
        row = jnp.broadcast_to(doc_row, (TOK, TOK))
        before = jnp.sum(jnp.where(row < doc2, 1.0, 0.0), axis=1, keepdims=True)
        token = lax.broadcasted_iota(jnp.int32, (TOK, HD), 0).astype(f32)
        position = token - before
        i = lax.broadcasted_iota(jnp.int32, (TOK, HD), 1)
        half = jnp.where(i < 64, i, i - 64).astype(f32)
        angle = position * jnp.exp(half * (-2.0 / HD * math.log(rope_base)))
        COS[...] = jnp.cos(angle)
        SIN[...] = jnp.where(i < 64, -1.0, 1.0) * jnp.sin(angle)
        u = lax.broadcasted_iota(jnp.int32, (TOK, TOK), 0)
        t = lax.broadcasted_iota(jnp.int32, (TOK, TOK), 1)
        bias = jnp.where((u <= t) & (row == doc2), 0.0, masked_score)
        BLO[...] = jnp.concatenate([bias[0:128, 0:128]] * 4, axis=1)
        BHI[...] = jnp.concatenate([bias[:, 128:256]] * 4, axis=1)

    def inverse():
        ld_x.wait()
        ld_xo.wait()
        a = X[0:TOK, :].astype(f32)
        total = jnp.sum(a * a, axis=1, keepdims=True)
        b = XO[...].astype(f32)
        total = total + jnp.sum(b * b, axis=1, keepdims=True)
        INV[...] = jnp.broadcast_to(lax.rsqrt(total * (1.0 / WIDE) + epsilon), (TOK, HD))
        CO[...] = jnp.zeros_like(CO)

    def transpose_x(who, j):
        XT[j * PIECE : (j + 1) * PIECE, who * TOK : (who + 1) * TOK] = X[
            who * TOK : (who + 1) * TOK, j * PIECE : (j + 1) * PIECE
        ].T

    def p_copy(g):
        return remote(POUT.at[g], PIN.at[g], p_s.at[g], p_r.at[g], partner)

    def project_partner(g):
        POUT[g] = dot(X[TOK : 2 * TOK, :], WB[g]).astype(bf16)
        p_copy(g).start()

    def project_own(g):
        PRAW[g] = dot(X[0:TOK, :], WB[g])

    def e_copy(g):
        return remote(E.at[g, 0:TOK], E.at[g, TOK : 2 * TOK], e_s.at[g], e_r.at[g], partner)

    def group_start(g):
        p_copy(g).wait_recv()
        raw = PRAW[g] + PIN[g].astype(f32)
        PRAW[g] = raw
        inv = INV[...]
        k = raw[:, 0:HD] * inv
        k = k * COS[...] + pltpu.roll(k, 64, 1) * SIN[...]
        kb = k.astype(bf16)
        KB[...] = kb
        KT[g] = kb.T
        VB[...] = (raw[:, HD : 2 * HD] * inv).astype(bf16)
        DKA[...] = jnp.zeros_like(DKA)
        DVA[...] = jnp.zeros_like(DVA)

    def group_end(g):
        dk = DKA[...] * SCALE
        inv = INV[...]
        dk = dk * COS[...] - pltpu.roll(dk, 64, 1) * SIN[...]
        ek = (dk * inv).astype(bf16)
        ev = (DVA[...] * inv).astype(bf16)
        E[g, 0:TOK, 0:HD] = ek
        E[g, 0:TOK, HD : 2 * HD] = ev
        e_copy(g).start()
        raw = PRAW[g]
        part = ek.astype(f32) * raw[:, 0:HD] + ev.astype(f32) * raw[:, HD : 2 * HD]
        CO[...] += jnp.broadcast_to(jnp.sum(part, axis=1, keepdims=True), (TOK, HD))

    low_rows, high_rows = slice(0, 128), slice(128, 256)

    def softmax(s, w):
        top = jnp.max(s, axis=0, keepdims=True)
        e = jnp.exp2((s - top) * EXP2_SCALE)
        p = e * (1.0 / jnp.sum(e, axis=0, keepdims=True))
        pw = p * w
        delta = jnp.sum(pw, axis=0, keepdims=True)
        return p.astype(bf16), (pw - p * delta).astype(bf16)

    def heads(n):
        def rows_of(ref, rows):
            return jnp.concatenate(
                [ref[rows, pl.ds(al(n * QUAD + i * HD, HD), HD)] for i in range(4)], axis=0
            )

        q_high, d_high = rows_of(Q, high_rows), rows_of(DO, high_rows)
        q_low, d_low = rows_of(Q, low_rows), rows_of(DO, low_rows)
        kb, vb = KB[...], VB[...]
        s_high, w_high = dot_nt(kb, q_high) + BHI[...], dot_nt(vb, d_high)
        s_low, w_low = dot_nt(kb[low_rows], q_low) + BLO[...], dot_nt(vb[low_rows], d_low)
        p_high, ds_high = softmax(s_high, w_high)
        p_low, ds_low = softmax(s_low, w_low)
        DSH[n] = ds_high
        DSL[n] = ds_low
        DKA[...] += dot(ds_high, q_high)
        DVA[...] += dot(p_high, d_high)
        DKA[low_rows, :] += dot(ds_low, q_low)
        DVA[low_rows, :] += dot(p_low, d_low)

    def query_gradient(n):
        g = n // 2
        for rows, ds in ((high_rows, DSH[n]), (low_rows, DSL[n])):
            kt = KT[g] if rows is high_rows else KT[g, :, 0:128]
            dq = (dot(kt, ds) * SCALE).T.astype(bf16)
            for i in range(4):
                c = n * QUAD + i * HD
                dq_out[rows, c : c + HD] = dq[i * 128 : (i + 1) * 128]

    def rs_copy(d, g, c, s):
        i = ring_sem(d, g, c, s)
        return remote(SB.at[i], RB.at[i], rs_s.at[i], rs_r.at[i], (right, left)[d])

    def rs_step(d, g, c, s):
        far = hops(d, c) + 1 - s
        owner = ring_at(far if d == 0 else -far)
        i = ring_sem(d, g, c, s)
        total = dot(XT[pl.ds(al(owner * TOK + c * 128, 128), 128), :], E[g])
        if s > 1:
            rs_copy(d, g, c, s - 1).wait_recv()
            total = total + RB[i - 1].astype(f32)
        SB[i] = total.astype(bf16)
        rs_copy(d, g, c, s).start()

    def rs_end(g):
        total = dot(XT[pl.ds(al(z * TOK, TOK), TOK), :], E[g])
        came = []
        for c in (0, 1):
            for d in (0, 1):
                rs_copy(d, g, c, hops(d, c)).wait_recv()
            first, second = (RB[ring_sem(d, g, c, hops(d, c))].astype(f32) for d in (0, 1))
            came.append(first + second)
        total = total + jnp.concatenate(came, axis=0)
        ck, cv = g * HD, 512 + g * HD
        wide_gain = GC[...]
        tk, tv = total[:, 0:HD], total[:, HD : 2 * HD]
        dw_out[0, :, ck : ck + HD] = tk * wide_gain
        dw_out[0, :, cv : cv + HD] = tv * wide_gain
        part = tk * WR[:, ck : ck + HD].astype(f32) + tv * WR[:, cv : cv + HD].astype(f32)
        GT[...] += jnp.broadcast_to(jnp.sum(part, axis=1, keepdims=True), (TOK, HD))

    def u_copy(j):
        return remote(UOUT.at[j], UIN.at[j], u_s.at[j], u_r.at[j], partner)

    def upstream(first, j):
        rows = slice(j * PIECE, (j + 1) * PIECE)
        total = dot_nt(E[0, first : first + TOK], WB[0, rows])
        for g in range(1, GROUPS):
            total = total + dot_nt(E[g, first : first + TOK], WB[g, rows])
        return total

    def send_upstream(j):
        UOUT[j] = upstream(TOK, j).astype(bf16)
        u_copy(j).start()

    def finish(part, j, u):
        cols = slice(j * PIECE, (j + 1) * PIECE)
        x = X[0:TOK, cols] if part == 0 else XO[:, cols]
        c = CO[...]
        c = jnp.concatenate([c] * (PIECE // HD), axis=1)
        start = al((h if part == 0 else 1 - h) * HALF + j * PIECE, PIECE)
        dx_out[:, pl.ds(start, PIECE)] = (u - x.astype(f32) * c).astype(bf16)

    def outer(k):
        (outer_1, outer_2, outer_3, outer_4, outer_5, outer_6, outer_7)[k - 1]()

    def x_transpose(who, j):
        if who == 1 and j < PIECES - 1:
            x_copy(j).wait_recv()
        transpose_x(who, j)

    def start_group(g):
        if g == 0:
            ld_q.wait()
            ld_do.wait()
        group_start(g)

    def end_group(g):
        group_end(g)
        if g == GROUPS - 1:
            CO[...] = CO[...] * INV[...] * INV[...] * (1.0 / WIDE)

    def first_projection(g):
        if g == 0:
            x_copy(PIECES - 1).wait_recv()
        project_partner(g)

    def upstream_in(j):
        u_copy(j).wait_recv()
        finish(1, j, UIN[j].astype(f32))

    def drain_ring(copy, g):
        for d in (0, 1):
            for c in (0, 1):
                for s in range(1, hops(d, c) + 1):
                    copy(d, g, c, s).wait_send()

    def drain(k):
        if k == 0:
            for j in range(PIECES):
                x_copy(j).wait_send()

            def gathers(g, _):
                p_copy(g).wait_send()
                drain_ring(ag_send, g)
                return 0

            lax.fori_loop(0, GROUPS, gathers, 0)
        elif k == 1:

            def sums(g, _):
                drain_ring(rs_copy, g)
                return 0

            lax.fori_loop(0, 2, sums, 0)
            for g in range(GROUPS):
                e_copy(g).wait_send()
            for c in (o_frag, o_state, o_y, o_pack, o_back_y, o_back_s):
                c.wait_send()
            for j in range(3):
                o_x(j).wait_send()
                o_back_x(j).wait_send()
        else:
            drain_ring(rs_copy, 2)

    acts = dict(
        ag=ag_step, own=ag_own, tab=tables, inv=inverse, tr=x_transpose, pp=first_projection, po=project_own,
        gs=start_group, ge=end_group, rs=rs_step, ew=lambda g: e_copy(g).wait_recv(), re=rs_end, us=send_upstream,
        uo=lambda j: finish(0, j, upstream(0, j)), ui=upstream_in, o=outer, dq=query_gradient, dr=drain,
    )

    def play(items):
        for name, *numbers in items:
            acts[name](*numbers)

    GT[...] = jnp.zeros_like(GT)
    play(BEFORE)

    def step(n, _):
        for k, items in enumerate(DURING):
            if items:

                @pl.when(n == k)
                def _(items=items):
                    play(items)

        heads(n)
        return 0

    lax.fori_loop(0, GROUPS * 2, step, 0)
    play(AFTER)
    spread = jnp.where(eye, jnp.concatenate([GT[...], GT[...]], axis=1), 0.0)
    dg_out[...] = jnp.sum(spread, axis=0, keepdims=True)

    drain_ring(rs_copy, 3)
    for j in range(PIECES):
        u_copy(j).wait_send()


def store(*refs):
    n = len(refs) // 2
    sems = refs[-1]
    copies = []
    for src, dst in zip(refs[:n], refs[n : 2 * n]):
        parts = STORE_PARTS if math.prod(src.shape) >= 2**18 else 1
        rows = src.shape[-2] // parts
        for i in range(parts):
            at = (slice(i * rows, (i + 1) * rows),) if parts > 1 else ()
            at = (0, *at) if parts > 1 and len(src.shape) == 3 else at
            a, b = (src.at[at], dst.at[at]) if at else (src, dst)
            copies.append(pltpu.make_async_copy(a, b, sems.at[len(copies)]))
    for c in copies:
        c.start()
    for c in copies:
        c.wait()


def on_device(x, q, do, doc, gain, w, fl, fm, fmo):
    sds = jax.ShapeDtypeStruct
    hbm = pl.BlockSpec(memory_space=pltpu.HBM)
    anywhere = pl.BlockSpec(memory_space=pl.ANY)
    vmem = pl.BlockSpec(memory_space=pltpu.VMEM)

    def v(shape, t):
        return pltpu.VMEM(shape, t)

    dma = pltpu.SemaphoreType.DMA
    scratch = [
        v((2 * TOK, HALF), bf16),
        v((TOK, HALF), bf16),
        v((HALF, 2 * TOK), bf16),
        v((TOK, WIDE), bf16),
        v((TOK, WIDE), bf16),
        v((TOK, 1024), bf16),
        v((GROUPS, HALF, 256), bf16),
        v((GROUPS, TOK, 256), bf16),
        v((GROUPS, TOK, 256), bf16),
        v((GROUPS, TOK, 256), f32),
        v((GROUPS, 2 * TOK, 256), bf16),
        v((PIECES, TOK, PIECE), bf16),
        v((PIECES, TOK, PIECE), bf16),
        v((64, 128, 256), bf16),
        v((64, 128, 256), bf16),
        v((TOK, HD), f32),
        v((TOK, HD), f32),
        v((TOK, HD), f32),
        v((TOK, HD), f32),
        v((128, 512), f32),
        v((256, 512), f32),
        v((8, 256, 512), bf16),
        v((8, 128, 512), bf16),
        v((TOK, HD), bf16),
        v((TOK, HD), bf16),
        v((GROUPS, HD, TOK), bf16),
        v((TOK, HD), f32),
        v((TOK, HD), f32),
        v((TOK, HD), f32),
        v((TOK, HD), f32),
        v((256, 1024), bf16),
        v((128, 1024), bf16),
        v((128, 1024), bf16),
        v((3, 128, 256), bf16),
        v((128, 128), bf16),
        v((128, 128), bf16),
        v((256, 1024), bf16),
        v((128, 256), f32),
        v((256, 128), f32),
        v((128, 128), f32),
        v((128, 128), f32),
        v((128, 128), f32),
        v((256, 128), f32),
        v((1, 256), jnp.int32),
        v((1, 256), bf16),
        dma((64,)), dma((64,)), dma((64,)), dma((64,)),
        dma((4,)), dma((4,)), dma((4,)), dma((4,)),
        dma((4,)), dma((4,)), dma((4,)), dma((4,)),
        dma((12,)), dma((12,)), dma((10,)),
    ]
    shapes = (
        sds((TOK, WIDE), bf16),
        sds((TOK, WIDE), bf16),
        sds((1, 256, 1024), f32),
        sds((1, 256), f32),
        sds((64, 256), f32),
        sds((64, 256), f32),
        sds((1, 256, 1024), bf16),
    )
    results = pl.pallas_call(
        kernel,
        out_shape=tuple(pltpu.VMEM(a.shape, a.dtype) for a in shapes),
        in_specs=[hbm] * 9,
        out_specs=(vmem,) * 7,
        scratch_shapes=scratch,
        compiler_params=pltpu.CompilerParams(
            collective_id=0, has_side_effects=True, vmem_limit_bytes=VMEM_LIMIT
        ),
        name="step",
    )(*(pltpu.with_memory_space_constraint(a, pltpu.HBM) for a in (x, q, do, doc, gain, w, fl, fm.T, fmo.T)))
    dq, dx, dw, dg, mn, mo, fn = pl.pallas_call(
        store,
        out_shape=shapes,
        in_specs=[anywhere] * 7,
        out_specs=(hbm,) * 7,
        scratch_shapes=[dma((3 + 4 * STORE_PARTS,))],
        compiler_params=pltpu.CompilerParams(vmem_limit_bytes=2**20),
        name="store",
    )(*results)
    return dq, dx, dw, dg, mn.T, mo.T, fn


def solution(mesh):
    placed = (
        P(("rep", "fsdp"), None),
        P(("rep", "fsdp"), None),
        P(("rep", "fsdp"), None),
        P(("rep", "fsdp"), None),
        P("rep", "fsdp"),
        P("rep", "fsdp", None),
        P("rep", "fsdp", None),
        P("fsdp", "rep"),
        P("fsdp", "rep"),
    )
    return jax.shard_map(
        on_device,
        mesh=mesh,
        in_specs=placed,
        out_specs=(
            P(("rep", "fsdp"), None),
            P(("rep", "fsdp"), None),
            P("rep", "fsdp", None),
            P("rep", "fsdp"),
            P("fsdp", "rep"),
            P("fsdp", "rep"),
            P("rep", "fsdp", None),
        ),
        check_vma=False,
    )
```
